32 devices in a mesh: dp: 8 (over z, x), tensor: 4 (over y, core).
Axes of the slice: x: 2, y: 2, z: 4, core: 2. Of those that a mesh axis runs over, the one named last changes fastest.
Arguments:
- inputs: bfloat16 [4096, 768], P(('dp', 'tensor')), may hold values from -6 to 6
- seq_lengths: int32 [8, 2], P('dp'), may hold values from 0 to 512, as said below
- attn_gain: bfloat16 [768], P('dp'), may hold values from 0.25 to 1.75
- wqkv: bfloat16 [768, 3, 768], P('dp', None, 'tensor'), may hold values from -0.21875 to 0.21875
- wo: bfloat16 [768, 768], P('tensor', 'dp'), may hold values from -2.5 to 2.5
- mlp_gain: bfloat16 [768], P('dp'), may hold values from 0.25 to 1.75
- wi: bfloat16 [768, 2, 1152], P('dp', None, 'tensor'), may hold values from -0.21875 to 0.21875
- wo2: bfloat16 [1152, 768], P('tensor', 'dp'), may hold values from -0.1875 to 0.1875
- cotangent: bfloat16 [4096, 768], P(('dp', 'tensor')), may hold values from -6 to 6
Outputs:
- output: bfloat16 [4096, 768], P(('dp', 'tensor'))
- input_grad: bfloat16 [4096, 768], P(('dp', 'tensor'))
- attn_gain_grad: float32 [768], P('dp')
- wqkv_grad: float32 [768, 3, 768], P('dp', None, 'tensor')
- wo_grad: float32 [768, 768], P('tensor', 'dp')
- mlp_gain_grad: float32 [768], P('dp')
- wi_grad: float32 [768, 2, 1152], P('dp', None, 'tensor')
- wo2_grad: float32 [1152, 768], P('tensor', 'dp')
The draws below stay inside these ranges and needn't reach their ends.
Inputs may be any that keep to these rules, and one draw needn't show every extreme that they name: Row g of seq_lengths lists the sequences packed from the first row of group g on; the lengths of a row sum to at most 512. In one row a single sequence fills all 512 rows and the other length is 0.
All inputs are finite; a program needn't handle non-finite values.
Results may differ from the reference program's by a relative error of at most 0.02.
Values may be sent and summed in bfloat16 or wider, within the bound.
A program may use at most 64 MiB of HBM per device.

```python
import jax
import jax.numpy as jnp
from jax import lax

D = 768
HEADS = 12
HEAD_DIM = 64
FF = 1152
SEQS = 2
GROUP = 512
TOKENS = 4096
N_DP = 8


def draw_seq_lengths(key, part):
    key = jax.random.fold_in(key, 11)
    key_long, key_short, key_pick, key_order = jax.random.split(key, 4)
    long_lengths = jax.random.randint(key_long, (N_DP,), 13 * GROUP // 16, 15 * GROUP // 16 + 1, dtype=jnp.int32)
    short_lengths = jax.random.randint(key_short, (N_DP,), GROUP // 16, GROUP - long_lengths + 1, dtype=jnp.int32)
    chosen = jax.random.randint(key_pick, (), 0, N_DP, dtype=jnp.int32)
    group_ids = jnp.arange(N_DP, dtype=jnp.int32)
    long_lengths = jnp.where(group_ids == chosen, GROUP, long_lengths).astype(jnp.int32)
    short_lengths = jnp.where(group_ids == chosen, 0, short_lengths).astype(jnp.int32)
    long_first = jax.random.randint(key_order, (N_DP,), 0, 2, dtype=jnp.int32)
    first_col = jnp.where(long_first == 1, long_lengths, short_lengths).astype(jnp.int32)
    second_col = jnp.where(long_first == 1, short_lengths, long_lengths).astype(jnp.int32)
    return jnp.stack([first_col, second_col], axis=1).astype(jnp.int32)


def spiked(array, own_key, source, target, blocks, factor):
    def block_of(dim):
        return (jnp.arange(array.shape[dim]) // (array.shape[dim] // blocks)).reshape((-1,) + (1,) * (array.ndim - 1 - dim))

    near = jax.random.permutation(own_key, blocks)[block_of(target)]
    far = (block_of(target) + blocks // 2) % blocks
    return jnp.where((block_of(source) == near) | (block_of(source) == far), factor * array, array)


def block_levels(own_key, shape, shards, smallest, largest):
    level, own = 1.0, jax.random.fold_in(own_key, 6)
    for dim, shards_of in shards:
        heights = jnp.exp(jax.random.uniform(jax.random.fold_in(own, dim), (shards_of,), jnp.float32, smallest / len(shards), largest / len(shards)))
        level = level * jnp.repeat(heights, shape[dim] // shards_of).reshape([-1 if axis == dim else 1 for axis in range(len(shape))])
    return level


def bell_draw(stream_key, dims, scale, limit, shards=(), kind=jnp.bfloat16):
    drawn = scale * jax.random.normal(stream_key, dims, jnp.float32)
    if shards:
        drawn = drawn * block_levels(stream_key, dims, shards, -0.22, 0.18)
    return jnp.clip(drawn, -limit, limit).astype(kind)


def heavy_noise(stream_key, dims, scale, most, cuts, heavy, kind=jnp.bfloat16):
    entries = scale * jax.random.normal(stream_key, dims, jnp.float32)
    if cuts:
        entries = entries * block_levels(stream_key, dims, cuts, -0.22, 0.18)
    return jnp.clip(spiked(entries, jax.random.fold_in(stream_key, 3), *heavy), -most, most).astype(kind)


def setup_inputs(seed: int = 0) -> dict:
    key_list = jax.random.split(jax.random.key(seed), 10)
    inputs = bell_draw(key_list[0], (TOKENS, D), 1.0, 6.0, ((0, 32),))
    seq_lengths = draw_seq_lengths(jax.random.fold_in(key_list[9], 71), 0)
    attn_gain = jnp.clip(1.0 + 0.15 * jax.random.normal(key_list[2], (D,), jnp.float32), 0.25, 1.75).astype(jnp.bfloat16)
    wqkv = bell_draw(key_list[3], (D, 3, D), D ** -0.5, 0.21875, ((0, 8), (2, 4)))
    wo = bell_draw(key_list[4], (D, D), (max(1, 4 * D // GROUP)) ** -0.5, 2.5, ((0, 4), (1, 8)))
    mlp_gain = jnp.clip(1.0 + 0.15 * jax.random.normal(key_list[5], (D,), jnp.float32), 0.25, 1.75).astype(jnp.bfloat16)
    wi = bell_draw(key_list[6], (D, 2, FF), D ** -0.5, 0.21875, ((0, 8), (2, 4)))
    wo2 = bell_draw(key_list[7], (FF, D), FF ** -0.5, 0.1875, ((0, 4), (1, 8)))
    cotangent = heavy_noise(key_list[8], (TOKENS, D), 1.0, 6.0, ((0, 32),), (0, 1, 32, 2.75))
    return {"inputs": inputs, "seq_lengths": seq_lengths, "attn_gain": attn_gain, "wqkv": wqkv, "wo": wo, "mlp_gain": mlp_gain, "wi": wi, "wo2": wo2, "cotangent": cotangent}


NORM_EPS = 1e-05
ROPE_THETA = 160000.0
SCORE_SCALE = 0.125
TOP_PRECISION = lax.Precision.HIGHEST

@jax.custom_vjp
def low(v):
    return lax.optimization_barrier(v.astype(jnp.bfloat16)).astype(jnp.float32)

@jax.custom_vjp
def low_back(v):
    return v

def low_keep(v):
    return (low(v), None)

def low_pass(kept, grad):
    return (grad,)

def back_keep(v):
    return (v, None)

def back_low(kept, grad):
    return (low(grad),)
low.defvjp(low_keep, low_pass)
low_back.defvjp(back_keep, back_low)

def layout(lengths, row_count):
    lengths = lengths.astype(jnp.int32)
    seq_ends = jnp.cumsum(lengths).astype(jnp.int32)
    row_ids = jnp.arange(row_count, dtype=jnp.int32)
    segment = lax.optimization_barrier(jnp.sum((row_ids[None, :] >= seq_ends[:, None]).astype(jnp.int32), axis=0)).astype(jnp.int32)
    starts = jnp.concatenate([seq_ends - lengths, seq_ends[-1:]]).astype(jnp.int32)
    slot_ids = jnp.arange(lengths.shape[0] + 1, dtype=jnp.int32)
    seq_begin = lax.optimization_barrier(jnp.sum(jnp.where(segment[None, :] == slot_ids[:, None], starts[:, None], 0), axis=0)).astype(jnp.int32)
    return (segment, (row_ids - seq_begin).astype(jnp.int32))

def normalize(array_in, gain_vec):
    row_mean = lax.optimization_barrier(jnp.mean(array_in, axis=-1, keepdims=True))
    centred = array_in - row_mean
    spread = lax.optimization_barrier(jnp.mean(centred * centred, axis=-1, keepdims=True))
    return centred * lax.rsqrt(spread + NORM_EPS) * gain_vec

def rotation(position):
    half_dim = HEAD_DIM // 2
    frequency = ROPE_THETA ** (-jnp.arange(half_dim, dtype=jnp.float32) / half_dim)
    angles = position.astype(jnp.float32)[:, None] * frequency[None, :]
    return (jnp.cos(angles)[:, None, :], jnp.sin(angles)[:, None, :])

def rotate(array_in, cosine, sine_table):
    half_dim = HEAD_DIM // 2
    first_half = array_in[..., :half_dim]
    second_half = array_in[..., half_dim:]
    return jnp.concatenate([first_half * cosine - second_half * sine_table, second_half * cosine + first_half * sine_table], axis=-1)

def attention_block(query_part, segment_part, key_all, value_all, segment):
    scores = jnp.einsum('qhd,khd->hqk', query_part, key_all, precision=TOP_PRECISION) * SCORE_SCALE
    scores = low_back(scores)
    same_seq = segment_part[:, None] == segment[None, :]
    scores = jnp.where(same_seq[None], scores, -1e+30)
    weights = jax.nn.softmax(scores, axis=-1)
    return jnp.einsum('hqk,khd->qhd', low(weights), value_all, precision=TOP_PRECISION)

def layer(inputs, weight_set, segment, position, valid_rows):
    attn_gain, wqkv, wo, mlp_gain, wi, wo2 = weight_set
    row_count = inputs.shape[0]
    attn_in = low(normalize(inputs, attn_gain))
    qkv = low_back(jnp.dot(attn_in, wqkv.reshape(D, 3 * D), precision=TOP_PRECISION)).reshape(row_count, 3, HEADS, HEAD_DIM)
    cosine, sine_table = rotation(position)
    query_low = low(rotate(qkv[:, 0], cosine, sine_table))
    key_low = low(rotate(qkv[:, 1], cosine, sine_table))
    value_low = low(qkv[:, 2])
    block_rows = min(512, row_count)
    block_count = row_count // block_rows
    block_step = jax.checkpoint(lambda pieces: attention_block(pieces[0], pieces[1], key_low, value_low, segment))
    context = lax.map(block_step, (query_low.reshape(block_count, block_rows, HEADS, HEAD_DIM), segment.reshape(block_count, block_rows)))
    context = low_back(low(context.reshape(row_count, D)))
    attn_out = low_back(jnp.dot(context, wo, precision=TOP_PRECISION))
    residual = inputs + attn_out
    mlp_in = low(normalize(residual, mlp_gain))
    projected = low_back(jnp.dot(mlp_in, wi.reshape(D, 2 * FF), precision=TOP_PRECISION)).reshape(row_count, 2, FF)
    hidden = low(jax.nn.gelu(projected[:, 0], approximate=False) * projected[:, 1])
    mlp_out = low_back(jnp.dot(hidden, wo2, precision=TOP_PRECISION))
    return valid_rows * (residual + mlp_out)

def reference(inputs, seq_lengths, attn_gain, wqkv, wo, mlp_gain, wi, wo2, cotangent):
    params = (attn_gain.astype(jnp.float32), wqkv.astype(jnp.float32), wo.astype(jnp.float32), mlp_gain.astype(jnp.float32), wi.astype(jnp.float32), wo2.astype(jnp.float32))
    x_groups = inputs.reshape(N_DP, GROUP, D)
    cot_groups = cotangent.reshape(N_DP, GROUP, D)

    def one_group(totals, pieces):
        group_in, group_cot, lengths = pieces
        segment, position = layout(lengths, GROUP)
        valid_rows = (segment < SEQS).astype(jnp.float32)[:, None]
        result, pull_back = jax.vjp(lambda group_x, weight_set: layer(group_x, weight_set, segment, position, valid_rows), group_in.astype(jnp.float32), params)
        grad_x, grad_weights = pull_back(group_cot.astype(jnp.float32))
        totals = jax.tree.map(lambda acc_sum, new_term: acc_sum + new_term, totals, grad_weights)
        return (totals, (result.astype(jnp.bfloat16), grad_x.astype(jnp.bfloat16)))
    zero_set = jax.tree.map(jnp.zeros_like, params)
    totals, (outputs, grads) = lax.scan(one_group, zero_set, (x_groups, cot_groups, seq_lengths))
    return (outputs.reshape(TOKENS, D), grads.reshape(TOKENS, D), totals[0], totals[1], totals[2], totals[3], totals[4], totals[5])
```

```python
import functools

import jax
import jax.numpy as jnp
from jax import lax
from jax.experimental import pallas as pl
from jax.experimental.pallas import tpu as pltpu
from jax.sharding import PartitionSpec as P

HEAD_DIM = 64
SEQS = 2
NORM_EPS = 1e-05
ROPE_THETA = 160000.0
SCORE_SCALE = 0.125
MESH = pl.DeviceIdType.MESH
GAIN_ROWS = 16


def layout(lengths, row_count):
    seq_ends = jnp.cumsum(lengths)
    row_ids = jnp.arange(row_count, dtype=jnp.int32)
    segment = jnp.sum((row_ids[None, :] >= seq_ends[:, None]).astype(jnp.int32), axis=0)
    starts = jnp.concatenate([seq_ends - lengths, seq_ends[-1:]])
    slot_ids = jnp.arange(lengths.shape[0] + 1, dtype=jnp.int32)
    seq_begin = jnp.sum(
        jnp.where(segment[None, :] == slot_ids[:, None], starts[:, None], 0), axis=0
    )
    return (segment, row_ids - seq_begin)


def unit_rows(array_in):
    row_mean = jnp.mean(array_in, axis=-1, keepdims=True)
    centred = array_in - row_mean
    spread = jnp.mean(centred * centred, axis=-1, keepdims=True)
    inverse = lax.rsqrt(spread + NORM_EPS)
    return centred * inverse, inverse


def norm_back(unit, inverse, gain, grad):
    pulled = grad * gain
    mean_pull = jnp.mean(pulled, axis=-1, keepdims=True)
    mean_both = jnp.mean(pulled * unit, axis=-1, keepdims=True)
    return (pulled - mean_pull - unit * mean_both) * inverse


def rotation(position):
    half_dim = HEAD_DIM // 2
    frequency = ROPE_THETA ** (-jnp.arange(half_dim, dtype=jnp.float32) / half_dim)
    angles = position.astype(jnp.float32)[:, None] * frequency[None, :]
    return (jnp.cos(angles)[:, None, :], jnp.sin(angles)[:, None, :])


def rotate(array_in, cosine, sine_table):
    half_dim = HEAD_DIM // 2
    first_half = array_in[..., :half_dim]
    second_half = array_in[..., half_dim:]
    return jnp.concatenate(
        [
            first_half * cosine - second_half * sine_table,
            second_half * cosine + first_half * sine_table,
        ],
        axis=-1,
    )


def places(n_dp, n_t):
    me = lax.axis_index("dp")
    rank = lax.axis_index("tensor")
    return me, rank


def greet(n_dp, n_t, me, rank):
    barrier = pltpu.get_barrier_semaphore()
    for step in range(1, n_t):
        pl.semaphore_signal(
            barrier, inc=1, device_id={"tensor": lax.rem(rank + step, n_t)}, device_id_type=MESH
        )
    for step in range(1, n_dp):
        pl.semaphore_signal(
            barrier, inc=1, device_id={"dp": lax.rem(me + step, n_dp)}, device_id_type=MESH
        )
    pl.semaphore_wait(barrier, n_dp + n_t - 2)


def send(src, dst, send_sem, recv_sem, device):
    copy = pltpu.make_async_remote_copy(
        src_ref=src,
        dst_ref=dst,
        send_sem=send_sem,
        recv_sem=recv_sem,
        device_id=device,
        device_id_type=MESH,
    )
    copy.start()
    return copy


class DpGather:
    def __init__(self, n_dp, me, own, full, sems):
        self.n_outer = n_dp // 2
        self.full, self.sems = full, sems
        self.outer, self.inner = lax.div(me, 2), lax.rem(me, 2)
        self.partner = {"dp": me + 1 - 2 * self.inner}
        full[me] = own[...]
        self.first, self.second = [], []
        for step in range(1, self.n_outer):
            peer = lax.rem(self.outer + step, self.n_outer) * 2 + self.inner
            self.first.append(
                send(full.at[me], full.at[me], sems.at[0, step], sems.at[1, step], {"dp": peer})
            )
        self.second.append(
            send(full.at[me], full.at[me], sems.at[2, 0], sems.at[3, 0], self.partner)
        )

    def forward(self):
        for step in range(1, self.n_outer):
            self.first[step - 1].wait_recv()
            source = lax.rem(self.outer + self.n_outer - step, self.n_outer) * 2 + self.inner
            self.second.append(
                send(
                    self.full.at[source],
                    self.full.at[source],
                    self.sems.at[2, step],
                    self.sems.at[3, step],
                    self.partner,
                )
            )

    def finish(self):
        for copy in self.second:
            copy.wait_recv()
        for copy in self.first + self.second:
            copy.wait_send()


class DpReduce:
    def __init__(self, n_dp, me, parts, pair, sums, far, sems):
        self.n_outer = n_dp // 2
        self.me, self.parts, self.pair, self.sums, self.far, self.sems = (
            me, parts, pair, sums, far, sems,
        )
        self.outer, self.inner = lax.div(me, 2), lax.rem(me, 2)
        partner = {"dp": me + 1 - 2 * self.inner}
        self.first, self.second = {}, {}
        for step in list(range(1, self.n_outer)) + [0]:
            block = lax.rem(self.outer + step, self.n_outer) * 2 + 1 - self.inner
            self.first[step] = send(
                parts.at[block], pair.at[step], sems.at[0, step], sems.at[1, step], partner
            )

    def forward(self):
        for step in range(1, self.n_outer):
            self.first[step].wait_recv()
            peer = lax.rem(self.outer + step, self.n_outer) * 2 + self.inner
            self.sums[step] = (
                self.parts[peer].astype(jnp.float32) + self.pair[step].astype(jnp.float32)
            ).astype(jnp.bfloat16)
            self.second[step] = send(
                self.sums.at[step],
                self.far.at[step],
                self.sems.at[2, step],
                self.sems.at[3, step],
                {"dp": peer},
            )

    def finish(self, out):
        self.first[0].wait_recv()
        total = self.parts[self.me].astype(jnp.float32) + self.pair[0].astype(jnp.float32)
        for step in range(1, self.n_outer):
            self.second[step].wait_recv()
            total = total + self.far[step].astype(jnp.float32)
        out[...] = total
        for copy in list(self.first.values()) + list(self.second.values()):
            copy.wait_send()


def start_rows_sum(n_t, rank, parts, slots, sems):
    copies = []
    for step in range(1, n_t):
        peer = lax.rem(rank + step, n_t)
        copies.append(
            send(parts.at[peer], slots.at[step - 1], sems.at[0, step], sems.at[1, step],
                 {"tensor": peer})
        )
    return copies


def end_rows_sum(n_t, rank, parts, slots, copies):
    total = parts[rank].astype(jnp.float32)
    for step in range(1, n_t):
        copies[step - 1].wait_recv()
        total = total + slots[step - 1].astype(jnp.float32)
    return total


def start_rows_gather(n_t, rank, full, sems):
    return [
        send(full.at[rank], full.at[rank], sems.at[0, step], sems.at[1, step],
             {"tensor": lax.rem(rank + step, n_t)})
        for step in range(1, n_t)
    ]


def end_sends(copies):
    for copy in copies:
        copy.wait_send()


def end_all(copies):
    for copy in copies:
        copy.wait_recv()
    end_sends(copies)


def gather_kernel(n_dp, n_t, w_ref, x_ref, cot_ref, w_all, x_all, cot_all, w_sems, x_sems, cot_sems):
    me, rank = places(n_dp, n_t)
    x_all[rank] = x_ref[...]
    cot_all[rank] = cot_ref[...]
    greet(n_dp, n_t, me, rank)
    weights = DpGather(n_dp, me, w_ref, w_all, w_sems)
    x_copies = start_rows_gather(n_t, rank, x_all, x_sems)
    cot_copies = start_rows_gather(n_t, rank, cot_all, cot_sems)
    weights.forward()
    end_all(x_copies)
    end_all(cot_copies)
    weights.finish()


def middle_kernel(
    n_dp, n_t, w_ref, part_ref, x_ref, gain_ref, w_all, residual_ref, mlp_all,
    slots, w_sems, part_sems, row_sems,
):
    me, rank = places(n_dp, n_t)
    greet(n_dp, n_t, me, rank)
    part_copies = start_rows_sum(n_t, rank, part_ref, slots, part_sems)
    weights = DpGather(n_dp, me, w_ref, w_all, w_sems)
    total = end_rows_sum(n_t, rank, part_ref, slots, part_copies)
    residual = x_ref[...].astype(jnp.float32) + total
    residual_ref[...] = residual
    unit, unused_inverse = unit_rows(residual)
    mlp_all[rank] = (unit * gain_ref[...]).astype(jnp.bfloat16)
    row_copies = start_rows_gather(n_t, rank, mlp_all, row_sems)
    weights.forward()
    end_all(row_copies)
    end_sends(part_copies)
    weights.finish()


def turn_kernel(
    n_dp, n_t, grads_ref, back_ref, out_part_ref, residual_ref, gain_ref, cot_ref, valid_ref,
    w_sum, output_ref, grad_residual_ref, grad_all, gain_part,
    back_slots, out_slots, pair, sums, far, back_sems, out_sems, w_sems, row_sems,
):
    me, rank = places(n_dp, n_t)
    greet(n_dp, n_t, me, rank)
    back_copies = start_rows_sum(n_t, rank, back_ref, back_slots, back_sems)
    weights = DpReduce(n_dp, me, grads_ref, pair, sums, far, w_sems)
    grad = end_rows_sum(n_t, rank, back_ref, back_slots, back_copies)
    residual = residual_ref[...]
    valid = valid_ref[...]
    unit, inverse = unit_rows(residual)
    gain_part[...] = jnp.sum(grad * unit, axis=0, keepdims=True)
    grad_residual = valid * cot_ref[...].astype(jnp.float32) + norm_back(
        unit, inverse, gain_ref[...], grad
    )
    grad_residual_ref[...] = grad_residual
    grad_all[rank] = grad_residual.astype(jnp.bfloat16)
    row_copies = start_rows_gather(n_t, rank, grad_all, row_sems)
    out_copies = start_rows_sum(n_t, rank, out_part_ref, out_slots, out_sems)
    weights.forward()
    end_all(row_copies)
    mlp_out = end_rows_sum(n_t, rank, out_part_ref, out_slots, out_copies)
    output_ref[...] = (valid * (residual + mlp_out)).astype(jnp.bfloat16)
    end_sends(back_copies)
    end_sends(out_copies)
    weights.finish(w_sum)


def last_kernel(
    n_dp, n_t, grads_ref, back_ref, x_ref, gain_ref, grad_residual_ref, gain_part_ref,
    w_sum, input_grad_ref, gain_sum_ref,
    back_slots, pair, sums, far, own_gain, near_gain, group_gain, far_gain,
    back_sems, w_sems, near_sems, far_sems,
):
    me, rank = places(n_dp, n_t)
    greet(n_dp, n_t, me, rank)
    back_copies = start_rows_sum(n_t, rank, back_ref, back_slots, back_sems)
    weights = DpReduce(n_dp, me, grads_ref, pair, sums, far, w_sems)
    grad = end_rows_sum(n_t, rank, back_ref, back_slots, back_copies)
    unit, inverse = unit_rows(x_ref[...].astype(jnp.float32))
    width = unit.shape[1]
    own_gain[0:1, :] = jnp.sum(grad * unit, axis=0, keepdims=True)
    own_gain[1:2, :] = gain_part_ref[...]
    own_gain[2:8, :] = jnp.zeros((6, width), jnp.float32)
    near = [
        send(own_gain, near_gain.at[step - 1], near_sems.at[0, step], near_sems.at[1, step],
             {"tensor": lax.rem(rank + step, n_t)})
        for step in range(1, n_t)
    ]
    input_grad_ref[...] = (
        grad_residual_ref[...] + norm_back(unit, inverse, gain_ref[...], grad)
    ).astype(jnp.bfloat16)
    total = own_gain[...]
    for step in range(1, n_t):
        near[step - 1].wait_recv()
        total = total + near_gain[step - 1]
    group_gain[...] = total
    far_copies = [
        send(group_gain, far_gain.at[step - 1], far_sems.at[0, step], far_sems.at[1, step],
             {"dp": lax.rem(me + step, n_dp)})
        for step in range(1, n_dp)
    ]
    weights.forward()
    for step in range(1, n_dp):
        far_copies[step - 1].wait_recv()
        total = total + far_gain[step - 1]
    gain_sum_ref[...] = total
    end_sends(near)
    end_sends(far_copies)
    end_sends(back_copies)
    weights.finish(w_sum)


def call(kernel, n_dp, n_t, number, outs, scratch, operands):
    in_vmem = pl.BlockSpec(memory_space=pltpu.VMEM)
    moved = sum(op.size * op.dtype.itemsize for op in operands)
    return pl.pallas_call(
        functools.partial(kernel, n_dp, n_t),
        out_shape=[jax.ShapeDtypeStruct(shape, kind) for shape, kind in outs],
        in_specs=[in_vmem] * len(operands),
        out_specs=[in_vmem] * len(outs),
        scratch_shapes=scratch,
        compiler_params=pltpu.CompilerParams(
            collective_id=number, has_side_effects=True, vmem_limit_bytes=40 * 2**20
        ),
        cost_estimate=pl.CostEstimate(flops=0, bytes_accessed=2 * moved, transcendentals=0),
    )(*operands)


def dot(first, second, dims):
    return lax.dot_general(first, second, (dims, ((), ())), preferred_element_type=jnp.float32)


def shards(inputs, seq_lengths, attn_gain, wqkv, wo, mlp_gain, wi, wo2, cotangent):
    low = jnp.bfloat16
    n_dp, n_t = lax.axis_size("dp"), lax.axis_size("tensor")
    me, rank = lax.axis_index("dp"), lax.axis_index("tensor")
    local_rows, width = inputs.shape
    group_rows = local_rows * n_t
    depth = wqkv.shape[0]
    head_cols = wqkv.shape[2]
    heads_here = head_cols // HEAD_DIM
    hidden_cols = wi.shape[2]
    first_cols = 3 * head_cols + wo.shape[0]
    second_cols = 2 * hidden_cols + wo2.shape[0]
    n_outer = n_dp // 2

    def dma(count):
        return pltpu.SemaphoreType.DMA(count)

    def row_sems():
        return dma((2, n_t))

    segment, position = layout(seq_lengths[0], group_rows)
    valid_all = (segment < SEQS).astype(jnp.float32)[:, None]
    valid_rows = lax.dynamic_slice_in_dim(valid_all, rank * local_rows, local_rows)
    cosine, sine_table = rotation(position)

    gain_row = jnp.concatenate([attn_gain, mlp_gain])
    gain_block = jnp.zeros((GAIN_ROWS, first_cols), low).at[0, : 2 * depth].set(gain_row)
    first_block = jnp.concatenate(
        [jnp.concatenate([wqkv.reshape(depth, 3 * head_cols), wo.T], axis=1), gain_block], axis=0
    )
    second_block = jnp.concatenate([wi.reshape(depth, 2 * hidden_cols), wo2.T], axis=1)

    first_all, x_all, cot_all = call(
        gather_kernel, n_dp, n_t, 1,
        [
            ((n_dp,) + first_block.shape, low),
            ((n_t, local_rows, width), low),
            ((n_t, local_rows, width), low),
        ],
        [dma((4, n_outer)), row_sems(), row_sems()],
        (first_block, inputs, cotangent),
    )
    full_qkv = first_all[:, :depth, : 3 * head_cols].reshape(width, 3 * head_cols)
    full_wo = first_all[:, :depth, 3 * head_cols :].reshape(width, wo.shape[0])
    gain_one = first_all[:, depth, :depth].reshape(1, width).astype(jnp.float32)
    gain_two = first_all[:, depth, depth : 2 * depth].reshape(1, width).astype(jnp.float32)
    grad_mlp_all = (
        valid_all * cot_all.reshape(group_rows, width).astype(jnp.float32)
    ).astype(low)

    unit, unused_inverse = unit_rows(x_all.reshape(group_rows, width).astype(jnp.float32))
    attn_all = (unit * gain_one).astype(low)
    qkv = dot(attn_all, full_qkv, ((1,), (0,))).reshape(group_rows, 3, heads_here, HEAD_DIM)
    query_low = rotate(qkv[:, 0], cosine, sine_table).astype(low)
    key_low = rotate(qkv[:, 1], cosine, sine_table).astype(low)
    value_low = qkv[:, 2].astype(low)
    scores = (
        jnp.einsum("qhd,khd->hqk", query_low, key_low, preferred_element_type=jnp.float32)
        * SCORE_SCALE
    )
    scores = jnp.where((segment[:, None] == segment[None, :])[None], scores, -1e30)
    exponent = jnp.exp(scores - jnp.max(scores, axis=-1, keepdims=True))
    probs = exponent / jnp.sum(exponent, axis=-1, keepdims=True)
    prob_low = probs.astype(low)
    context = (
        jnp.einsum("hqk,khd->qhd", prob_low, value_low, preferred_element_type=jnp.float32)
        .astype(low)
        .reshape(group_rows, head_cols)
    )
    attn_part = dot(context, full_wo, ((1,), (1,))).astype(low)

    row_block = (n_t, local_rows, width)
    slots = pltpu.VMEM((n_t - 1, local_rows, width), low)
    second_all, residual, mlp_all = call(
        middle_kernel, n_dp, n_t, 2,
        [
            ((n_dp,) + second_block.shape, low),
            ((local_rows, width), jnp.float32),
            (row_block, low),
        ],
        [slots, dma((4, n_outer)), row_sems(), row_sems()],
        (second_block, attn_part.reshape(row_block), inputs, gain_two),
    )
    full_wi = second_all[:, :, : 2 * hidden_cols].reshape(width, 2 * hidden_cols)
    full_wo2 = second_all[:, :, 2 * hidden_cols :].reshape(width, wo2.shape[0])
    mlp_all = mlp_all.reshape(group_rows, width)
    projected = dot(mlp_all, full_wi, ((1,), (0,)))
    gate, other = projected[:, :hidden_cols], projected[:, hidden_cols:]
    bell = 0.5 * (1.0 + lax.erf(gate * 0.7071067811865476))
    gelu = gate * bell
    slope = bell + gate * jnp.exp(-0.5 * gate * gate) * 0.3989422804014327
    hidden = (gelu * other).astype(low)
    out_part = dot(hidden, full_wo2, ((1,), (1,))).astype(low)
    grad_hidden = dot(grad_mlp_all, full_wo2, ((1,), (0,)))
    grad_proj = jnp.concatenate(
        [grad_hidden * other * slope, grad_hidden * gelu], axis=1
    ).astype(low)
    back_part = dot(grad_proj, full_wi, ((1,), (1,))).astype(low)
    second_grads = jnp.concatenate(
        [
            dot(mlp_all, grad_proj, ((0,), (0,))).astype(low),
            dot(grad_mlp_all, hidden, ((0,), (0,))).astype(low),
        ],
        axis=1,
    ).reshape(n_dp, depth, second_cols)

    def reduce_scratch(cols):
        return [pltpu.VMEM((n_outer, depth, cols), low)] * 3

    second_sum, output, grad_residual, grad_all, gain_part = call(
        turn_kernel, n_dp, n_t, 3,
        [
            ((depth, second_cols), jnp.float32),
            ((local_rows, width), low),
            ((local_rows, width), jnp.float32),
            (row_block, low),
            ((1, width), jnp.float32),
        ],
        [slots, slots] + reduce_scratch(second_cols)
        + [row_sems(), row_sems(), dma((4, n_outer)), row_sems()],
        (
            second_grads, back_part.reshape(row_block), out_part.reshape(row_block),
            residual, gain_two, cotangent, valid_rows,
        ),
    )
    grad_all = grad_all.reshape(group_rows, width)
    grad_context = dot(grad_all, full_wo, ((1,), (0,))).astype(low)
    grad_context = grad_context.reshape(group_rows, heads_here, HEAD_DIM)
    grad_value = jnp.einsum(
        "hqk,qhd->khd", prob_low, grad_context, preferred_element_type=jnp.float32
    )
    grad_probs = jnp.einsum(
        "qhd,khd->hqk", grad_context, value_low, preferred_element_type=jnp.float32
    )
    row_inner = jnp.sum(probs * grad_probs, axis=-1, keepdims=True)
    grad_scores = (probs * (grad_probs - row_inner)).astype(low)
    grad_query = (
        jnp.einsum("hqk,khd->qhd", grad_scores, key_low, preferred_element_type=jnp.float32)
        * SCORE_SCALE
    )
    grad_key = (
        jnp.einsum("hqk,qhd->khd", grad_scores, query_low, preferred_element_type=jnp.float32)
        * SCORE_SCALE
    )
    grad_qkv = jnp.stack(
        [
            rotate(grad_query, cosine, -sine_table),
            rotate(grad_key, cosine, -sine_table),
            grad_value,
        ],
        axis=1,
    )
    grad_qkv = grad_qkv.astype(low).reshape(group_rows, 3 * head_cols)
    first_grads = jnp.concatenate(
        [
            dot(attn_all, grad_qkv, ((0,), (0,))).astype(low),
            dot(grad_all, context, ((0,), (0,))).astype(low),
        ],
        axis=1,
    ).reshape(n_dp, depth, first_cols)
    attn_back = dot(grad_qkv, full_qkv, ((1,), (1,))).astype(low)

    gain_block_f32 = pltpu.VMEM((8, width), jnp.float32)
    first_sum, input_grad, gain_sum = call(
        last_kernel, n_dp, n_t, 4,
        [
            ((depth, first_cols), jnp.float32),
            ((local_rows, width), low),
            ((8, width), jnp.float32),
        ],
        [slots] + reduce_scratch(first_cols)
        + [
            gain_block_f32,
            pltpu.VMEM((n_t - 1, 8, width), jnp.float32),
            gain_block_f32,
            pltpu.VMEM((n_dp - 1, 8, width), jnp.float32),
            row_sems(), dma((4, n_outer)), row_sems(), dma((2, n_dp)),
        ],
        (
            first_grads, attn_back.reshape(row_block), inputs, gain_one, grad_residual, gain_part,
        ),
    )
    gains_here = lax.dynamic_slice_in_dim(gain_sum[:2], me * depth, depth, axis=1)
    return (
        output,
        input_grad,
        gains_here[0],
        first_sum[:, : 3 * head_cols].reshape(depth, 3, head_cols),
        first_sum[:, 3 * head_cols :].T,
        gains_here[1],
        second_sum[:, : 2 * hidden_cols].reshape(depth, 2, hidden_cols),
        second_sum[:, 2 * hidden_cols :].T,
    )


def solution(mesh):
    in_specs = (
        P(("dp", "tensor"), None),
        P("dp", None),
        P("dp"),
        P("dp", None, "tensor"),
        P("tensor", "dp"),
        P("dp"),
        P("dp", None, "tensor"),
        P("tensor", "dp"),
        P(("dp", "tensor"), None),
    )
    out_specs = (
        P(("dp", "tensor"), None),
        P(("dp", "tensor"), None),
        P("dp"),
        P("dp", None, "tensor"),
        P("tensor", "dp"),
        P("dp"),
        P("dp", None, "tensor"),
        P("tensor", "dp"),
    )
    return jax.shard_map(shards, mesh=mesh, in_specs=in_specs, out_specs=out_specs, check_vma=False)
```

```python
import functools

import jax
import jax.numpy as jnp
from jax import lax
from jax.experimental import pallas as pl
from jax.experimental.pallas import tpu as pltpu
from jax.sharding import PartitionSpec as P

HEAD_DIM = 64
SEQS = 2
NORM_EPS = 1e-05
ROPE_THETA = 160000.0
SCORE_SCALE = 0.125
MESH = pl.DeviceIdType.MESH
GAIN_ROWS = 16


def layout(lengths, row_count):
    seq_ends = jnp.cumsum(lengths)
    row_ids = jnp.arange(row_count, dtype=jnp.int32)
    segment = jnp.sum((row_ids[None, :] >= seq_ends[:, None]).astype(jnp.int32), axis=0)
    starts = jnp.concatenate([seq_ends - lengths, seq_ends[-1:]])
    slot_ids = jnp.arange(lengths.shape[0] + 1, dtype=jnp.int32)
    seq_begin = jnp.sum(
        jnp.where(segment[None, :] == slot_ids[:, None], starts[:, None], 0), axis=0
    )
    return (segment, row_ids - seq_begin)


def unit_rows(array_in):
    row_mean = jnp.mean(array_in, axis=-1, keepdims=True)
    centred = array_in - row_mean
    spread = jnp.mean(centred * centred, axis=-1, keepdims=True)
    inverse = lax.rsqrt(spread + NORM_EPS)
    return centred * inverse, inverse


def norm_back(unit, inverse, gain, grad):
    pulled = grad * gain
    mean_pull = jnp.mean(pulled, axis=-1, keepdims=True)
    mean_both = jnp.mean(pulled * unit, axis=-1, keepdims=True)
    return (pulled - mean_pull - unit * mean_both) * inverse


def rotation(position):
    half_dim = HEAD_DIM // 2
    frequency = ROPE_THETA ** (-jnp.arange(half_dim, dtype=jnp.float32) / half_dim)
    angles = position.astype(jnp.float32)[:, None] * frequency[None, :]
    return (jnp.cos(angles)[:, None, :], jnp.sin(angles)[:, None, :])


def rotate(array_in, cosine, sine_table):
    half_dim = HEAD_DIM // 2
    first_half = array_in[..., :half_dim]
    second_half = array_in[..., half_dim:]
    return jnp.concatenate(
        [
            first_half * cosine - second_half * sine_table,
            second_half * cosine + first_half * sine_table,
        ],
        axis=-1,
    )


def flip(index):
    return index + 1 - 2 * lax.rem(index, 2)


def greet(n_dp, n_t, me, rank, all_dp=False):
    barrier = pltpu.get_barrier_semaphore()
    peers = [{"tensor": lax.rem(rank + step, n_t)} for step in range(1, n_t)]
    if all_dp:
        peers += [{"dp": lax.rem(me + step, n_dp)} for step in range(1, n_dp)]
    else:
        peers += [{"dp": lax.rem(me + 2 * step, n_dp)} for step in range(1, n_dp // 2)]
        peers += [{"dp": flip(me)}]
    for peer in peers:
        pl.semaphore_signal(barrier, inc=1, device_id=peer, device_id_type=MESH)
    pl.semaphore_wait(barrier, len(peers))


def send(src, dst, send_sem, recv_sem, device):
    copy = pltpu.make_async_remote_copy(
        src_ref=src,
        dst_ref=dst,
        send_sem=send_sem,
        recv_sem=recv_sem,
        device_id=device,
        device_id_type=MESH,
    )
    copy.start()
    return copy


class Gather:
    def __init__(self, axis, count, me, full, sems):
        self.axis, self.count, self.me, self.full, self.sems = axis, count, me, full, sems
        self.n_outer = count // 2
        self.first, self.second = {}, {}
        for step in range(1, self.n_outer):
            peer = {axis: lax.rem(me + 2 * step, count)}
            self.first[step] = send(
                full.at[me], full.at[me], sems.at[0, step], sems.at[1, step], peer
            )
        self.hand_on(0, me)

    def hand_on(self, step, block):
        self.second[step] = send(
            self.full.at[block],
            self.full.at[block],
            self.sems.at[2, step],
            self.sems.at[3, step],
            {self.axis: flip(self.me)},
        )

    def forward(self, step):
        self.first[step].wait_recv()
        self.hand_on(step, lax.rem(self.me + self.count - 2 * step, self.count))

    def finish(self):
        for copy in self.second.values():
            copy.wait_recv()
        for copy in list(self.first.values()) + list(self.second.values()):
            copy.wait_send()


class Reduce:
    def __init__(self, axis, count, me, parts, pair, sums, far, sems):
        self.axis, self.count, self.me, self.parts = axis, count, me, parts
        self.pair, self.sums, self.far, self.sems = pair, sums, far, sems
        self.n_outer = count // 2
        self.first, self.second = {}, {}
        for step in list(range(1, self.n_outer)) + [0]:
            block = lax.rem(flip(me) + 2 * step, count)
            self.first[step] = send(
                parts.at[block], pair.at[step], sems.at[0, step], sems.at[1, step],
                {axis: flip(me)},
            )

    def forward(self, step):
        self.first[step].wait_recv()
        peer = lax.rem(self.me + 2 * step, self.count)
        self.sums[step] = (
            self.parts[peer].astype(jnp.float32) + self.pair[step].astype(jnp.float32)
        ).astype(jnp.bfloat16)
        self.second[step] = send(
            self.sums.at[step],
            self.far.at[step],
            self.sems.at[2, step],
            self.sems.at[3, step],
            {self.axis: peer},
        )

    def total(self):
        self.first[0].wait_recv()
        total = self.parts[self.me].astype(jnp.float32) + self.pair[0].astype(jnp.float32)
        for step in range(1, self.n_outer):
            self.second[step].wait_recv()
            total = total + self.far[step].astype(jnp.float32)
        return total

    def finish(self):
        for copy in list(self.first.values()) + list(self.second.values()):
            copy.wait_send()


def forward_all(stages, first=1):
    last = max(stage.n_outer for stage in stages)
    for step in range(first, last):
        for stage in stages:
            if step not in stage.second and step < stage.n_outer:
                stage.forward(step)


def gather_kernel(n_dp, n_t, w_ref, x_ref, cot_ref, w_all, x_all, cot_all, w_sems, x_sems, cot_sems):
    me, rank = lax.axis_index("dp"), lax.axis_index("tensor")
    w_all[me] = w_ref[...]
    x_all[rank] = x_ref[...]
    cot_all[rank] = cot_ref[...]
    greet(n_dp, n_t, me, rank)
    weights = Gather("dp", n_dp, me, w_all, w_sems)
    x_rows = Gather("tensor", n_t, rank, x_all, x_sems)
    cot_rows = Gather("tensor", n_t, rank, cot_all, cot_sems)
    forward_all([weights, x_rows])
    forward_all([cot_rows])
    x_rows.finish()
    cot_rows.finish()
    weights.finish()


def middle_kernel(
    n_dp, n_t, w_ref, part_ref, x_ref, gain_ref, w_all, residual_ref, mlp_all,
    pair, sums, far, w_sems, part_sems, row_sems,
):
    me, rank = lax.axis_index("dp"), lax.axis_index("tensor")
    w_all[me] = w_ref[...]
    greet(n_dp, n_t, me, rank)
    parts = Reduce("tensor", n_t, rank, part_ref, pair, sums, far, part_sems)
    weights = Gather("dp", n_dp, me, w_all, w_sems)
    forward_all([parts])
    weights.forward(1)
    residual = x_ref[...].astype(jnp.float32) + parts.total()
    residual_ref[...] = residual
    unit, unused_inverse = unit_rows(residual)
    mlp_all[rank] = (unit * gain_ref[...]).astype(jnp.bfloat16)
    rows = Gather("tensor", n_t, rank, mlp_all, row_sems)
    weights.forward(2)
    forward_all([rows])
    forward_all([weights])
    rows.finish()
    parts.finish()
    weights.finish()


def turn_kernel(
    n_dp, n_t, grads_ref, back_ref, out_part_ref, residual_ref, gain_ref, cot_ref, valid_ref,
    w_sum, output_ref, grad_residual_ref, grad_all, gain_part,
    back_pair, back_sums, back_far, out_pair, out_sums, out_far, pair, sums, far,
    back_sems, out_sems, w_sems, row_sems,
):
    me, rank = lax.axis_index("dp"), lax.axis_index("tensor")
    greet(n_dp, n_t, me, rank)
    back = Reduce("tensor", n_t, rank, back_ref, back_pair, back_sums, back_far, back_sems)
    weights = Reduce("dp", n_dp, me, grads_ref, pair, sums, far, w_sems)
    forward_all([back])
    mlp_out = Reduce("tensor", n_t, rank, out_part_ref, out_pair, out_sums, out_far, out_sems)
    weights.forward(1)
    grad = back.total()
    residual = residual_ref[...]
    valid = valid_ref[...]
    unit, inverse = unit_rows(residual)
    gain_part[...] = jnp.sum(grad * unit, axis=0, keepdims=True)
    grad_residual = valid * cot_ref[...].astype(jnp.float32) + norm_back(
        unit, inverse, gain_ref[...], grad
    )
    grad_residual_ref[...] = grad_residual
    grad_all[rank] = grad_residual.astype(jnp.bfloat16)
    rows = Gather("tensor", n_t, rank, grad_all, row_sems)
    weights.forward(2)
    forward_all([mlp_out])
    forward_all([rows])
    forward_all([weights])
    output_ref[...] = (valid * (residual + mlp_out.total())).astype(jnp.bfloat16)
    rows.finish()
    back.finish()
    mlp_out.finish()
    w_sum[...] = weights.total()
    weights.finish()


def last_kernel(
    n_dp, n_t, grads_ref, back_ref, x_ref, gain_ref, grad_residual_ref, gain_part_ref,
    w_sum, input_grad_ref, gain_sum_ref,
    back_pair, back_sums, back_far, pair, sums, far, own_gain, near_gain, group_gain, far_gain,
    back_sems, w_sems, near_sems, far_sems,
):
    me, rank = lax.axis_index("dp"), lax.axis_index("tensor")
    greet(n_dp, n_t, me, rank, all_dp=True)
    back = Reduce("tensor", n_t, rank, back_ref, back_pair, back_sums, back_far, back_sems)
    weights = Reduce("dp", n_dp, me, grads_ref, pair, sums, far, w_sems)
    forward_all([back])
    weights.forward(1)
    grad = back.total()
    unit, inverse = unit_rows(x_ref[...].astype(jnp.float32))
    width = unit.shape[1]
    own_gain[0:1, :] = jnp.sum(grad * unit, axis=0, keepdims=True)
    own_gain[1:2, :] = gain_part_ref[...]
    own_gain[2:8, :] = jnp.zeros((6, width), jnp.float32)
    near = [
        send(own_gain, near_gain.at[step - 1], near_sems.at[0, step], near_sems.at[1, step],
             {"tensor": lax.rem(rank + step, n_t)})
        for step in range(1, n_t)
    ]
    weights.forward(2)
    input_grad_ref[...] = (
        grad_residual_ref[...] + norm_back(unit, inverse, gain_ref[...], grad)
    ).astype(jnp.bfloat16)
    total = own_gain[...]
    for step in range(1, n_t):
        near[step - 1].wait_recv()
        total = total + near_gain[step - 1]
    group_gain[...] = total
    far_copies = [
        send(group_gain, far_gain.at[step - 1], far_sems.at[0, step], far_sems.at[1, step],
             {"dp": lax.rem(me + step, n_dp)})
        for step in range(1, n_dp)
    ]
    forward_all([weights])
    for step in range(1, n_dp):
        far_copies[step - 1].wait_recv()
        total = total + far_gain[step - 1]
    gain_sum_ref[...] = total
    for copy in near + far_copies:
        copy.wait_send()
    back.finish()
    w_sum[...] = weights.total()
    weights.finish()


def call(kernel, n_dp, n_t, number, outs, scratch, operands):
    in_vmem = pl.BlockSpec(memory_space=pltpu.VMEM)
    moved = sum(op.size * op.dtype.itemsize for op in operands)
    return pl.pallas_call(
        functools.partial(kernel, n_dp, n_t),
        out_shape=[jax.ShapeDtypeStruct(shape, kind) for shape, kind in outs],
        in_specs=[in_vmem] * len(operands),
        out_specs=[in_vmem] * len(outs),
        scratch_shapes=scratch,
        compiler_params=pltpu.CompilerParams(
            collective_id=number, has_side_effects=True, vmem_limit_bytes=40 * 2**20
        ),
        cost_estimate=pl.CostEstimate(flops=0, bytes_accessed=2 * moved, transcendentals=0),
    )(*operands)


def dot(first, second, dims):
    return lax.dot_general(first, second, (dims, ((), ())), preferred_element_type=jnp.float32)


def shards(inputs, seq_lengths, attn_gain, wqkv, wo, mlp_gain, wi, wo2, cotangent):
    low = jnp.bfloat16
    n_dp, n_t = lax.axis_size("dp"), lax.axis_size("tensor")
    me, rank = lax.axis_index("dp"), lax.axis_index("tensor")
    local_rows, width = inputs.shape
    group_rows = local_rows * n_t
    depth = wqkv.shape[0]
    head_cols = wqkv.shape[2]
    heads_here = head_cols // HEAD_DIM
    hidden_cols = wi.shape[2]
    first_cols = 3 * head_cols + wo.shape[0]
    second_cols = 2 * hidden_cols + wo2.shape[0]
    n_outer = n_dp // 2

    def dma(count):
        return pltpu.SemaphoreType.DMA(count)

    def row_sems():
        return dma((4, n_t // 2))

    segment, position = layout(seq_lengths[0], group_rows)
    valid_all = (segment < SEQS).astype(jnp.float32)[:, None]
    valid_rows = lax.dynamic_slice_in_dim(valid_all, rank * local_rows, local_rows)
    cosine, sine_table = rotation(position)

    gain_row = jnp.concatenate([attn_gain, mlp_gain])
    gain_block = jnp.zeros((GAIN_ROWS, first_cols), low).at[0, : 2 * depth].set(gain_row)
    first_block = jnp.concatenate(
        [jnp.concatenate([wqkv.reshape(depth, 3 * head_cols), wo.T], axis=1), gain_block], axis=0
    )
    second_block = jnp.concatenate([wi.reshape(depth, 2 * hidden_cols), wo2.T], axis=1)

    first_all, x_all, cot_all = call(
        gather_kernel, n_dp, n_t, 1,
        [
            ((n_dp,) + first_block.shape, low),
            ((n_t, local_rows, width), low),
            ((n_t, local_rows, width), low),
        ],
        [dma((4, n_outer)), row_sems(), row_sems()],
        (first_block, inputs, cotangent),
    )
    full_qkv = first_all[:, :depth, : 3 * head_cols].reshape(width, 3 * head_cols)
    full_wo = first_all[:, :depth, 3 * head_cols :].reshape(width, wo.shape[0])
    gain_one = first_all[:, depth, :depth].reshape(1, width).astype(jnp.float32)
    gain_two = first_all[:, depth, depth : 2 * depth].reshape(1, width).astype(jnp.float32)
    grad_mlp_all = (
        valid_all * cot_all.reshape(group_rows, width).astype(jnp.float32)
    ).astype(low)

    unit, unused_inverse = unit_rows(x_all.reshape(group_rows, width).astype(jnp.float32))
    attn_all = (unit * gain_one).astype(low)
    qkv = dot(attn_all, full_qkv, ((1,), (0,))).reshape(group_rows, 3, heads_here, HEAD_DIM)
    query_low = rotate(qkv[:, 0], cosine, sine_table).astype(low)
    key_low = rotate(qkv[:, 1], cosine, sine_table).astype(low)
    value_low = qkv[:, 2].astype(low)
    scores = (
        jnp.einsum("qhd,khd->hqk", query_low, key_low, preferred_element_type=jnp.float32)
        * SCORE_SCALE
    )
    scores = jnp.where((segment[:, None] == segment[None, :])[None], scores, -1e30)
    exponent = jnp.exp(scores - jnp.max(scores, axis=-1, keepdims=True))
    probs = exponent / jnp.sum(exponent, axis=-1, keepdims=True)
    prob_low = probs.astype(low)
    context = (
        jnp.einsum("hqk,khd->qhd", prob_low, value_low, preferred_element_type=jnp.float32)
        .astype(low)
        .reshape(group_rows, head_cols)
    )
    attn_part = dot(context, full_wo, ((1,), (1,))).astype(low)

    row_block = (n_t, local_rows, width)
    slots = [pltpu.VMEM((n_t // 2, local_rows, width), low)] * 3
    second_all, residual, mlp_all = call(
        middle_kernel, n_dp, n_t, 2,
        [
            ((n_dp,) + second_block.shape, low),
            ((local_rows, width), jnp.float32),
            (row_block, low),
        ],
        slots + [dma((4, n_outer)), row_sems(), row_sems()],
        (second_block, attn_part.reshape(row_block), inputs, gain_two),
    )
    full_wi = second_all[:, :, : 2 * hidden_cols].reshape(width, 2 * hidden_cols)
    full_wo2 = second_all[:, :, 2 * hidden_cols :].reshape(width, wo2.shape[0])
    mlp_all = mlp_all.reshape(group_rows, width)
    projected = dot(mlp_all, full_wi, ((1,), (0,)))
    gate, other = projected[:, :hidden_cols], projected[:, hidden_cols:]
    bell = 0.5 * (1.0 + lax.erf(gate * 0.7071067811865476))
    gelu = gate * bell
    slope = bell + gate * jnp.exp(-0.5 * gate * gate) * 0.3989422804014327
    hidden = (gelu * other).astype(low)
    out_part = dot(hidden, full_wo2, ((1,), (1,))).astype(low)
    grad_hidden = dot(grad_mlp_all, full_wo2, ((1,), (0,)))
    grad_proj = jnp.concatenate(
        [grad_hidden * other * slope, grad_hidden * gelu], axis=1
    ).astype(low)
    back_part = dot(grad_proj, full_wi, ((1,), (1,))).astype(low)
    second_grads = jnp.concatenate(
        [
            dot(mlp_all, grad_proj, ((0,), (0,))).astype(low),
            dot(grad_mlp_all, hidden, ((0,), (0,))).astype(low),
        ],
        axis=1,
    ).reshape(n_dp, depth, second_cols)

    def reduce_scratch(cols):
        return [pltpu.VMEM((n_outer, depth, cols), low)] * 3

    second_sum, output, grad_residual, grad_all, gain_part = call(
        turn_kernel, n_dp, n_t, 3,
        [
            ((depth, second_cols), jnp.float32),
            ((local_rows, width), low),
            ((local_rows, width), jnp.float32),
            (row_block, low),
            ((1, width), jnp.float32),
        ],
        slots + slots + reduce_scratch(second_cols)
        + [row_sems(), row_sems(), dma((4, n_outer)), row_sems()],
        (
            second_grads, back_part.reshape(row_block), out_part.reshape(row_block),
            residual, gain_two, cotangent, valid_rows,
        ),
    )
    grad_all = grad_all.reshape(group_rows, width)
    grad_context = dot(grad_all, full_wo, ((1,), (0,))).astype(low)
    grad_context = grad_context.reshape(group_rows, heads_here, HEAD_DIM)
    grad_value = jnp.einsum(
        "hqk,qhd->khd", prob_low, grad_context, preferred_element_type=jnp.float32
    )
    grad_probs = jnp.einsum(
        "qhd,khd->hqk", grad_context, value_low, preferred_element_type=jnp.float32
    )
    row_inner = jnp.sum(probs * grad_probs, axis=-1, keepdims=True)
    grad_scores = (probs * (grad_probs - row_inner)).astype(low)
    grad_query = (
        jnp.einsum("hqk,khd->qhd", grad_scores, key_low, preferred_element_type=jnp.float32)
        * SCORE_SCALE
    )
    grad_key = (
        jnp.einsum("hqk,qhd->khd", grad_scores, query_low, preferred_element_type=jnp.float32)
        * SCORE_SCALE
    )
    grad_qkv = jnp.stack(
        [
            rotate(grad_query, cosine, -sine_table),
            rotate(grad_key, cosine, -sine_table),
            grad_value,
        ],
        axis=1,
    )
    grad_qkv = grad_qkv.astype(low).reshape(group_rows, 3 * head_cols)
    first_grads = jnp.concatenate(
        [
            dot(attn_all, grad_qkv, ((0,), (0,))).astype(low),
            dot(grad_all, context, ((0,), (0,))).astype(low),
        ],
        axis=1,
    ).reshape(n_dp, depth, first_cols)
    attn_back = dot(grad_qkv, full_qkv, ((1,), (1,))).astype(low)

    gain_block_f32 = pltpu.VMEM((8, width), jnp.float32)
    first_sum, input_grad, gain_sum = call(
        last_kernel, n_dp, n_t, 4,
        [
            ((depth, first_cols), jnp.float32),
            ((local_rows, width), low),
            ((8, width), jnp.float32),
        ],
        slots + reduce_scratch(first_cols)
        + [
            gain_block_f32,
            pltpu.VMEM((n_t - 1, 8, width), jnp.float32),
            gain_block_f32,
            pltpu.VMEM((n_dp - 1, 8, width), jnp.float32),
            row_sems(), dma((4, n_outer)), dma((2, n_t)), dma((2, n_dp)),
        ],
        (
            first_grads, attn_back.reshape(row_block), inputs, gain_one, grad_residual, gain_part,
        ),
    )
    gains_here = lax.dynamic_slice_in_dim(gain_sum[:2], me * depth, depth, axis=1)
    return (
        output,
        input_grad,
        gains_here[0],
        first_sum[:, : 3 * head_cols].reshape(depth, 3, head_cols),
        first_sum[:, 3 * head_cols :].T,
        gains_here[1],
        second_sum[:, : 2 * hidden_cols].reshape(depth, 2, hidden_cols),
        second_sum[:, 2 * hidden_cols :].T,
    )


def solution(mesh):
    in_specs = (
        P(("dp", "tensor"), None),
        P("dp", None),
        P("dp"),
        P("dp", None, "tensor"),
        P("tensor", "dp"),
        P("dp"),
        P("dp", None, "tensor"),
        P("tensor", "dp"),
        P(("dp", "tensor"), None),
    )
    out_specs = (
        P(("dp", "tensor"), None),
        P(("dp", "tensor"), None),
        P("dp"),
        P("dp", None, "tensor"),
        P("tensor", "dp"),
        P("dp"),
        P("dp", None, "tensor"),
        P("tensor", "dp"),
    )
    return jax.shard_map(shards, mesh=mesh, in_specs=in_specs, out_specs=out_specs, check_vma=False)
```

```python
import functools

import jax
import jax.numpy as jnp
from jax import lax
from jax.experimental import pallas as pl
from jax.experimental.pallas import tpu as pltpu
from jax.sharding import PartitionSpec as P

HEAD_DIM = 64
SEQS = 2
NORM_EPS = 1e-05
ROPE_THETA = 160000.0
SCORE_SCALE = 0.125
MESH = pl.DeviceIdType.MESH
GAIN_ROWS = 16


def layout(lengths, row_count):
    row_ids = jnp.arange(row_count, dtype=jnp.int32)
    segment, begin, end = jnp.zeros_like(row_ids), jnp.zeros_like(row_ids), 0
    for slot in range(SEQS):
        end = end + lengths[slot]
        past = row_ids >= end
        segment = segment + past.astype(jnp.int32)
        begin = begin + jnp.where(past, lengths[slot], 0)
    return (segment, row_ids - begin)


def valid_mask(lengths_ref, first_row, row_count):
    used = lengths_ref[0, 0]
    for slot in range(1, SEQS):
        used = used + lengths_ref[0, slot]
    row_ids = lax.broadcasted_iota(jnp.int32, (row_count, 1), 0) + first_row
    return (row_ids < used).astype(jnp.float32)


def unit_rows(array_in):
    row_mean = jnp.mean(array_in, axis=-1, keepdims=True)
    centred = array_in - row_mean
    spread = jnp.mean(centred * centred, axis=-1, keepdims=True)
    inverse = lax.rsqrt(spread + NORM_EPS)
    return centred * inverse, inverse


def norm_back(unit, inverse, gain, grad):
    pulled = grad * gain
    mean_pull = jnp.mean(pulled, axis=-1, keepdims=True)
    mean_both = jnp.mean(pulled * unit, axis=-1, keepdims=True)
    return (pulled - mean_pull - unit * mean_both) * inverse


def rotation(position):
    half_dim = HEAD_DIM // 2
    frequency = ROPE_THETA ** (-jnp.arange(half_dim, dtype=jnp.float32) / half_dim)
    angles = position.astype(jnp.float32)[:, None] * frequency[None, :]
    return (jnp.cos(angles)[:, None, :], jnp.sin(angles)[:, None, :])


def rotate(array_in, cosine, sine_table):
    half_dim = HEAD_DIM // 2
    first_half = array_in[..., :half_dim]
    second_half = array_in[..., half_dim:]
    return jnp.concatenate(
        [
            first_half * cosine - second_half * sine_table,
            second_half * cosine + first_half * sine_table,
        ],
        axis=-1,
    )


def flip(index):
    return index + 1 - 2 * lax.rem(index, 2)


def greet(n_dp, n_t, me, rank, all_dp=False):
    barrier = pltpu.get_barrier_semaphore()
    peers = [{"tensor": lax.rem(rank + step, n_t)} for step in range(1, n_t)]
    if all_dp:
        peers += [{"dp": lax.rem(me + step, n_dp)} for step in range(1, n_dp)]
    else:
        peers += [{"dp": lax.rem(me + 2 * step, n_dp)} for step in range(1, n_dp // 2)]
        peers += [{"dp": flip(me)}]
    for peer in peers:
        pl.semaphore_signal(barrier, inc=1, device_id=peer, device_id_type=MESH)
    pl.semaphore_wait(barrier, len(peers))


def send(src, dst, send_sem, recv_sem, device):
    copy = pltpu.make_async_remote_copy(
        src_ref=src,
        dst_ref=dst,
        send_sem=send_sem,
        recv_sem=recv_sem,
        device_id=device,
        device_id_type=MESH,
    )
    copy.start()
    return copy


class Gather:
    def __init__(self, axis, count, me, full, sems):
        self.axis, self.count, self.me, self.full, self.sems = axis, count, me, full, sems
        self.n_outer = count // 2
        self.first, self.second = {}, {}
        for step in range(1, self.n_outer):
            peer = {axis: lax.rem(me + 2 * step, count)}
            self.first[step] = send(
                full.at[me], full.at[me], sems.at[0, step], sems.at[1, step], peer
            )
        self.hand_on(0, me)

    def hand_on(self, step, block):
        self.second[step] = send(
            self.full.at[block],
            self.full.at[block],
            self.sems.at[2, step],
            self.sems.at[3, step],
            {self.axis: flip(self.me)},
        )

    def forward(self, step):
        self.first[step].wait_recv()
        self.hand_on(step, lax.rem(self.me + self.count - 2 * step, self.count))

    def arrive(self):
        for copy in self.second.values():
            copy.wait_recv()

    def leave(self):
        for copy in list(self.first.values()) + list(self.second.values()):
            copy.wait_send()

    def finish(self):
        self.arrive()
        self.leave()


class Reduce:
    def __init__(self, axis, count, me, parts, pair, sums, far, sems, pieces=()):
        self.axis, self.count, self.me, self.parts = axis, count, me, parts
        self.pieces = pieces
        self.pair, self.sums, self.far, self.sems = pair, sums, far, sems
        self.n_outer = count // 2
        self.first, self.second = {}, {}
        for step in list(range(1, self.n_outer)) + [0]:
            block = lax.rem(flip(me) + 2 * step, count)
            self.pack(block)
            self.first[step] = send(
                parts.at[block], pair.at[step], sems.at[0, step], sems.at[1, step],
                {axis: flip(me)},
            )
        for step in range(self.n_outer):
            self.pack(lax.rem(me + 2 * step, count))

    def pack(self, block):
        column = 0
        for piece in self.pieces:
            width = piece.shape[2]
            self.parts[block, :, column : column + width] = piece[block]
            column += width

    def forward(self, step):
        self.first[step].wait_recv()
        peer = lax.rem(self.me + 2 * step, self.count)
        self.sums[step] = (
            self.parts[peer].astype(jnp.float32) + self.pair[step].astype(jnp.float32)
        ).astype(jnp.bfloat16)
        self.second[step] = send(
            self.sums.at[step],
            self.far.at[step],
            self.sems.at[2, step],
            self.sems.at[3, step],
            {self.axis: peer},
        )

    def total(self):
        self.first[0].wait_recv()
        total = self.parts[self.me].astype(jnp.float32) + self.pair[0].astype(jnp.float32)
        for step in range(1, self.n_outer):
            self.second[step].wait_recv()
            total = total + self.far[step].astype(jnp.float32)
        return total

    def finish(self):
        for copy in list(self.first.values()) + list(self.second.values()):
            copy.wait_send()


def forward_all(stages, first=1):
    last = max(stage.n_outer for stage in stages)
    for step in range(first, last):
        for stage in stages:
            if step not in stage.second and step < stage.n_outer:
                stage.forward(step)


def gather_kernel(
    n_dp, n_t, lengths_ref, w_ref, x_ref, cot_ref,
    qkv_all, wo_all, attn_all, grad_all, gain_one, gain_two,
    w_all, x_all, cot_all, units, w_sems, x_sems, cot_sems,
):
    me, rank = lax.axis_index("dp"), lax.axis_index("tensor")
    w_all[me] = w_ref[...]
    x_all[rank] = x_ref[...]
    cot_all[rank] = cot_ref[...]
    greet(n_dp, n_t, me, rank)
    weights = Gather("dp", n_dp, me, w_all, w_sems)
    x_rows = Gather("tensor", n_t, rank, x_all, x_sems)
    cot_rows = Gather("tensor", n_t, rank, cot_all, cot_sems)
    weights.forward(1)
    forward_all([x_rows, cot_rows])
    forward_all([weights])
    x_rows.arrive()
    cot_rows.arrive()
    row_count, width = x_ref.shape
    for block in range(n_t):
        unit, unused_inverse = unit_rows(x_all[block].astype(jnp.float32))
        units[block] = unit
        valid = valid_mask(lengths_ref, block * row_count, row_count)
        grad_all[block] = (valid * cot_all[block].astype(jnp.float32)).astype(jnp.bfloat16)
    weights.arrive()
    gains = jnp.sum(w_all[:, :GAIN_ROWS, :width].astype(jnp.float32), axis=0)
    gain_one[...] = gains[0:1]
    gain_two[...] = gains[1:2]
    for block in range(n_t):
        attn_all[block] = (units[block] * gains[0:1]).astype(jnp.bfloat16)
    split = qkv_all.shape[2]
    qkv_all[...] = w_all[:, GAIN_ROWS:, :split]
    wo_all[...] = w_all[:, GAIN_ROWS:, split:]
    x_rows.leave()
    cot_rows.leave()
    weights.leave()


def middle_kernel(
    n_dp, n_t, w_ref, part_ref, x_ref, gain_ref, w_all, residual_ref, mlp_all,
    pair, sums, far, w_sems, part_sems, row_sems,
):
    me, rank = lax.axis_index("dp"), lax.axis_index("tensor")
    w_all[me] = w_ref[...]
    greet(n_dp, n_t, me, rank)
    parts = Reduce("tensor", n_t, rank, part_ref, pair, sums, far, part_sems)
    weights = Gather("dp", n_dp, me, w_all, w_sems)
    forward_all([parts])
    weights.forward(1)
    residual = x_ref[...].astype(jnp.float32) + parts.total()
    residual_ref[...] = residual
    unit, unused_inverse = unit_rows(residual)
    mlp_all[rank] = (unit * gain_ref[...]).astype(jnp.bfloat16)
    rows = Gather("tensor", n_t, rank, mlp_all, row_sems)
    weights.forward(2)
    forward_all([rows])
    forward_all([weights])
    rows.finish()
    parts.finish()
    weights.finish()


def turn_kernel(
    n_dp, n_t, lengths_ref, piece_one, piece_two, back_ref, out_part_ref, residual_ref, gain_ref,
    cot_ref,
    w_sum, output_ref, grad_residual_ref, grad_all, gain_part,
    back_pair, back_sums, back_far, out_pair, out_sums, out_far, grads, pair, sums, far,
    back_sems, out_sems, w_sems, row_sems,
):
    me, rank = lax.axis_index("dp"), lax.axis_index("tensor")
    greet(n_dp, n_t, me, rank)
    back = Reduce("tensor", n_t, rank, back_ref, back_pair, back_sums, back_far, back_sems)
    weights = Reduce(
        "dp", n_dp, me, grads, pair, sums, far, w_sems, (piece_one, piece_two)
    )
    forward_all([back])
    mlp_out = Reduce("tensor", n_t, rank, out_part_ref, out_pair, out_sums, out_far, out_sems)
    weights.forward(1)
    grad = back.total()
    residual = residual_ref[...]
    row_count = residual.shape[0]
    valid = valid_mask(lengths_ref, rank * row_count, row_count)
    unit, inverse = unit_rows(residual)
    gain_part[...] = jnp.sum(grad * unit, axis=0, keepdims=True)
    grad_residual = valid * cot_ref[...].astype(jnp.float32) + norm_back(
        unit, inverse, gain_ref[...], grad
    )
    grad_residual_ref[...] = grad_residual
    grad_all[rank] = grad_residual.astype(jnp.bfloat16)
    rows = Gather("tensor", n_t, rank, grad_all, row_sems)
    weights.forward(2)
    forward_all([mlp_out])
    forward_all([rows])
    forward_all([weights])
    output_ref[...] = (valid * (residual + mlp_out.total())).astype(jnp.bfloat16)
    rows.finish()
    back.finish()
    mlp_out.finish()
    w_sum[...] = weights.total()
    weights.finish()


def last_kernel(
    n_dp, n_t, piece_one, piece_two, back_ref, x_ref, gain_ref, grad_residual_ref, gain_part_ref,
    w_sum, input_grad_ref, gain_sum_ref,
    back_pair, back_sums, back_far, grads, pair, sums, far, own_gain, near_gain, group_gain, far_gain,
    back_sems, w_sems, near_sems, far_sems,
):
    me, rank = lax.axis_index("dp"), lax.axis_index("tensor")
    greet(n_dp, n_t, me, rank, all_dp=True)
    back = Reduce("tensor", n_t, rank, back_ref, back_pair, back_sums, back_far, back_sems)
    weights = Reduce(
        "dp", n_dp, me, grads, pair, sums, far, w_sems, (piece_one, piece_two)
    )
    forward_all([back])
    weights.forward(1)
    grad = back.total()
    unit, inverse = unit_rows(x_ref[...].astype(jnp.float32))
    width = unit.shape[1]
    own_gain[0:1, :] = jnp.sum(grad * unit, axis=0, keepdims=True)
    own_gain[1:2, :] = gain_part_ref[...]
    own_gain[2:8, :] = jnp.zeros((6, width), jnp.float32)
    near = [
        send(own_gain, near_gain.at[step - 1], near_sems.at[0, step], near_sems.at[1, step],
             {"tensor": lax.rem(rank + step, n_t)})
        for step in range(1, n_t)
    ]
    weights.forward(2)
    input_grad_ref[...] = (
        grad_residual_ref[...] + norm_back(unit, inverse, gain_ref[...], grad)
    ).astype(jnp.bfloat16)
    total = own_gain[...]
    for step in range(1, n_t):
        near[step - 1].wait_recv()
        total = total + near_gain[step - 1]
    group_gain[...] = total
    far_copies = [
        send(group_gain, far_gain.at[step - 1], far_sems.at[0, step], far_sems.at[1, step],
             {"dp": lax.rem(me + step, n_dp)})
        for step in range(1, n_dp)
    ]
    forward_all([weights])
    for step in range(1, n_dp):
        far_copies[step - 1].wait_recv()
        total = total + far_gain[step - 1]
    gain_sum_ref[...] = total
    for copy in near + far_copies:
        copy.wait_send()
    back.finish()
    w_sum[...] = weights.total()
    weights.finish()


def call(kernel, n_dp, n_t, number, outs, scratch, operands):
    in_vmem = pl.BlockSpec(memory_space=pltpu.VMEM)
    moved = sum(op.size * op.dtype.itemsize for op in operands)
    return pl.pallas_call(
        functools.partial(kernel, n_dp, n_t),
        out_shape=[jax.ShapeDtypeStruct(shape, kind) for shape, kind in outs],
        in_specs=[
            pl.BlockSpec(memory_space=pltpu.SMEM) if op.dtype == jnp.int32 else in_vmem
            for op in operands
        ],
        out_specs=[in_vmem] * len(outs),
        scratch_shapes=scratch,
        compiler_params=pltpu.CompilerParams(
            collective_id=number, has_side_effects=True, vmem_limit_bytes=40 * 2**20
        ),
        cost_estimate=pl.CostEstimate(flops=0, bytes_accessed=2 * moved, transcendentals=0),
    )(*operands)


def dot(first, second, dims):
    return lax.dot_general(first, second, (dims, ((), ())), preferred_element_type=jnp.float32)


def shards(inputs, seq_lengths, attn_gain, wqkv, wo, mlp_gain, wi, wo2, cotangent):
    low = jnp.bfloat16
    n_dp, n_t = lax.axis_size("dp"), lax.axis_size("tensor")
    me, rank = lax.axis_index("dp"), lax.axis_index("tensor")
    local_rows, width = inputs.shape
    group_rows = local_rows * n_t
    depth = wqkv.shape[0]
    head_cols = wqkv.shape[2]
    heads_here = head_cols // HEAD_DIM
    hidden_cols = wi.shape[2]
    first_cols = 3 * head_cols + wo.shape[0]
    second_cols = 2 * hidden_cols + wo2.shape[0]
    n_outer = n_dp // 2

    def dma(count):
        return pltpu.SemaphoreType.DMA(count)

    def row_sems():
        return dma((4, n_t // 2))

    segment, position = layout(seq_lengths[0], group_rows)
    cosine, sine_table = rotation(position)

    gain_block = lax.dynamic_update_slice(
        jnp.zeros((GAIN_ROWS, first_cols), low), jnp.stack([attn_gain, mlp_gain]), (0, me * depth)
    )
    first_block = jnp.concatenate(
        [gain_block, jnp.concatenate([wqkv.reshape(depth, 3 * head_cols), wo.T], axis=1)], axis=0
    )
    second_block = jnp.concatenate([wi.reshape(depth, 2 * hidden_cols), wo2.T], axis=1)

    row_block = (n_t, local_rows, width)
    full_qkv, full_wo, attn_all, grad_mlp_all, gain_one, gain_two = call(
        gather_kernel, n_dp, n_t, 1,
        [
            ((n_dp, depth, 3 * head_cols), low),
            ((n_dp, depth, wo.shape[0]), low),
            (row_block, low),
            (row_block, low),
            ((1, width), jnp.float32),
            ((1, width), jnp.float32),
        ],
        [
            pltpu.VMEM((n_dp,) + first_block.shape, low),
            pltpu.VMEM(row_block, low),
            pltpu.VMEM(row_block, low),
            pltpu.VMEM(row_block, jnp.float32),
            dma((4, n_outer)), row_sems(), row_sems(),
        ],
        (seq_lengths, first_block, inputs, cotangent),
    )
    full_qkv = full_qkv.reshape(width, 3 * head_cols)
    full_wo = full_wo.reshape(width, wo.shape[0])
    attn_all = attn_all.reshape(group_rows, width)
    grad_mlp_all = grad_mlp_all.reshape(group_rows, width)
    qkv = dot(attn_all, full_qkv, ((1,), (0,))).reshape(group_rows, 3, heads_here, HEAD_DIM)
    query_low = rotate(qkv[:, 0], cosine, sine_table).astype(low)
    key_low = rotate(qkv[:, 1], cosine, sine_table).astype(low)
    value_low = qkv[:, 2].astype(low)
    scores = (
        jnp.einsum("qhd,khd->hqk", query_low, key_low, preferred_element_type=jnp.float32)
        * SCORE_SCALE
    )
    scores = jnp.where((segment[:, None] == segment[None, :])[None], scores, -1e30)
    exponent = jnp.exp(scores - jnp.max(scores, axis=-1, keepdims=True))
    probs = exponent / jnp.sum(exponent, axis=-1, keepdims=True)
    prob_low = probs.astype(low)
    context = (
        jnp.einsum("hqk,khd->qhd", prob_low, value_low, preferred_element_type=jnp.float32)
        .astype(low)
        .reshape(group_rows, head_cols)
    )
    attn_part = dot(context, full_wo, ((1,), (1,))).astype(low)

    slots = [pltpu.VMEM((n_t // 2, local_rows, width), low)] * 3
    second_all, residual, mlp_all = call(
        middle_kernel, n_dp, n_t, 2,
        [
            ((n_dp,) + second_block.shape, low),
            ((local_rows, width), jnp.float32),
            (row_block, low),
        ],
        slots + [dma((4, n_outer)), row_sems(), row_sems()],
        (second_block, attn_part.reshape(row_block), inputs, gain_two),
    )
    full_wi = second_all[:, :, : 2 * hidden_cols].reshape(width, 2 * hidden_cols)
    full_wo2 = second_all[:, :, 2 * hidden_cols :].reshape(width, wo2.shape[0])
    mlp_all = mlp_all.reshape(group_rows, width)
    projected = dot(mlp_all, full_wi, ((1,), (0,)))
    gate, other = projected[:, :hidden_cols], projected[:, hidden_cols:]
    bell = 0.5 * (1.0 + lax.erf(gate * 0.7071067811865476))
    gelu = gate * bell
    slope = bell + gate * jnp.exp(-0.5 * gate * gate) * 0.3989422804014327
    hidden = (gelu * other).astype(low)
    out_part = dot(hidden, full_wo2, ((1,), (1,))).astype(low)
    grad_hidden = dot(grad_mlp_all, full_wo2, ((1,), (0,)))
    grad_proj = jnp.concatenate(
        [grad_hidden * other * slope, grad_hidden * gelu], axis=1
    ).astype(low)
    back_part = dot(grad_proj, full_wi, ((1,), (1,))).astype(low)
    wi_grad = dot(mlp_all, grad_proj, ((0,), (0,))).astype(low)
    wo2_grad = dot(grad_mlp_all, hidden, ((0,), (0,))).astype(low)

    def reduce_scratch(cols):
        return [pltpu.VMEM((n_dp, depth, cols), low)] + [
            pltpu.VMEM((n_outer, depth, cols), low)
        ] * 3

    second_sum, output, grad_residual, grad_all, gain_part = call(
        turn_kernel, n_dp, n_t, 3,
        [
            ((depth, second_cols), jnp.float32),
            ((local_rows, width), low),
            ((local_rows, width), jnp.float32),
            (row_block, low),
            ((1, width), jnp.float32),
        ],
        slots + slots + reduce_scratch(second_cols)
        + [row_sems(), row_sems(), dma((4, n_outer)), row_sems()],
        (
            seq_lengths,
            wi_grad.reshape(n_dp, depth, 2 * hidden_cols),
            wo2_grad.reshape(n_dp, depth, wo2.shape[0]),
            back_part.reshape(row_block), out_part.reshape(row_block),
            residual, gain_two, cotangent,
        ),
    )
    grad_all = grad_all.reshape(group_rows, width)
    grad_context = dot(grad_all, full_wo, ((1,), (0,))).astype(low)
    grad_context = grad_context.reshape(group_rows, heads_here, HEAD_DIM)
    grad_value = jnp.einsum(
        "hqk,qhd->khd", prob_low, grad_context, preferred_element_type=jnp.float32
    )
    grad_probs = jnp.einsum(
        "qhd,khd->hqk", grad_context, value_low, preferred_element_type=jnp.float32
    )
    row_inner = jnp.sum(probs * grad_probs, axis=-1, keepdims=True)
    grad_scores = (probs * (grad_probs - row_inner)).astype(low)
    grad_query = (
        jnp.einsum("hqk,khd->qhd", grad_scores, key_low, preferred_element_type=jnp.float32)
        * SCORE_SCALE
    )
    grad_key = (
        jnp.einsum("hqk,qhd->khd", grad_scores, query_low, preferred_element_type=jnp.float32)
        * SCORE_SCALE
    )
    grad_qkv = jnp.stack(
        [
            rotate(grad_query, cosine, -sine_table),
            rotate(grad_key, cosine, -sine_table),
            grad_value,
        ],
        axis=1,
    )
    grad_qkv = grad_qkv.astype(low).reshape(group_rows, 3 * head_cols)
    wqkv_grad = dot(attn_all, grad_qkv, ((0,), (0,))).astype(low)
    wo_grad = dot(grad_all, context, ((0,), (0,))).astype(low)
    attn_back = dot(grad_qkv, full_qkv, ((1,), (1,))).astype(low)

    gain_block_f32 = pltpu.VMEM((8, width), jnp.float32)
    first_sum, input_grad, gain_sum = call(
        last_kernel, n_dp, n_t, 4,
        [
            ((depth, first_cols), jnp.float32),
            ((local_rows, width), low),
            ((8, width), jnp.float32),
        ],
        slots + reduce_scratch(first_cols)
        + [
            gain_block_f32,
            pltpu.VMEM((n_t - 1, 8, width), jnp.float32),
            gain_block_f32,
            pltpu.VMEM((n_dp - 1, 8, width), jnp.float32),
            row_sems(), dma((4, n_outer)), dma((2, n_t)), dma((2, n_dp)),
        ],
        (
            wqkv_grad.reshape(n_dp, depth, 3 * head_cols),
            wo_grad.reshape(n_dp, depth, wo.shape[0]),
            attn_back.reshape(row_block), inputs, gain_one, grad_residual, gain_part,
        ),
    )
    gains_here = lax.dynamic_slice_in_dim(gain_sum[:2], me * depth, depth, axis=1)
    return (
        output,
        input_grad,
        gains_here[0],
        first_sum[:, : 3 * head_cols].reshape(depth, 3, head_cols),
        first_sum[:, 3 * head_cols :].T,
        gains_here[1],
        second_sum[:, : 2 * hidden_cols].reshape(depth, 2, hidden_cols),
        second_sum[:, 2 * hidden_cols :].T,
    )


def solution(mesh):
    in_specs = (
        P(("dp", "tensor"), None),
        P("dp", None),
        P("dp"),
        P("dp", None, "tensor"),
        P("tensor", "dp"),
        P("dp"),
        P("dp", None, "tensor"),
        P("tensor", "dp"),
        P(("dp", "tensor"), None),
    )
    out_specs = (
        P(("dp", "tensor"), None),
        P(("dp", "tensor"), None),
        P("dp"),
        P("dp", None, "tensor"),
        P("tensor", "dp"),
        P("dp"),
        P("dp", None, "tensor"),
        P("tensor", "dp"),
    )
    return jax.shard_map(shards, mesh=mesh, in_specs=in_specs, out_specs=out_specs, check_vma=False)
```

```python
import functools

import jax
import jax.numpy as jnp
from jax import lax
from jax.experimental import pallas as pl
from jax.experimental.pallas import tpu as pltpu
from jax.sharding import PartitionSpec as P

HEAD_DIM = 64
SEQS = 2
NORM_EPS = 1e-05
ROPE_THETA = 160000.0
SCORE_SCALE = 0.125
MESH = pl.DeviceIdType.MESH
GAIN_ROWS = 16


def layout(lengths, row_count):
    slots = jnp.arange(SEQS, dtype=jnp.int32)
    ends = jnp.sum(jnp.where(slots[None, :] <= slots[:, None], lengths[None, :], 0), axis=1)
    row_ids = jnp.arange(row_count, dtype=jnp.int32)
    past = row_ids[None, :] >= ends[:, None]
    segment = jnp.sum(past.astype(jnp.int32), axis=0)
    begin = jnp.sum(jnp.where(past, lengths[:, None], 0), axis=0)
    return (segment, row_ids - begin)


def valid_mask(lengths_ref, first_row, row_count):
    used = lengths_ref[0, 0]
    for slot in range(1, SEQS):
        used = used + lengths_ref[0, slot]
    row_ids = lax.broadcasted_iota(jnp.int32, (row_count, 1), 0) + first_row
    return (row_ids < used).astype(jnp.float32)


def unit_rows(array_in):
    row_mean = jnp.mean(array_in, axis=-1, keepdims=True)
    centred = array_in - row_mean
    spread = jnp.mean(centred * centred, axis=-1, keepdims=True)
    inverse = lax.rsqrt(spread + NORM_EPS)
    return centred * inverse, inverse


def norm_back(unit, inverse, gain, grad):
    pulled = grad * gain
    mean_pull = jnp.mean(pulled, axis=-1, keepdims=True)
    mean_both = jnp.mean(pulled * unit, axis=-1, keepdims=True)
    return (pulled - mean_pull - unit * mean_both) * inverse


def rotation(position):
    half_dim = HEAD_DIM // 2
    frequency = ROPE_THETA ** (-jnp.arange(half_dim, dtype=jnp.float32) / half_dim)
    angles = position.astype(jnp.float32)[:, None] * frequency[None, :]
    return (jnp.cos(angles)[:, None, :], jnp.sin(angles)[:, None, :])


def rotate(array_in, cosine, sine_table):
    half_dim = HEAD_DIM // 2
    first_half = array_in[..., :half_dim]
    second_half = array_in[..., half_dim:]
    return jnp.concatenate(
        [
            first_half * cosine - second_half * sine_table,
            second_half * cosine + first_half * sine_table,
        ],
        axis=-1,
    )


def flip(index):
    return index + 1 - 2 * lax.rem(index, 2)


def greet(n_dp, n_t, me, rank, all_dp=False):
    barrier = pltpu.get_barrier_semaphore()
    peers = [{"tensor": lax.rem(rank + step, n_t)} for step in range(1, n_t)]
    if all_dp:
        peers += [{"dp": lax.rem(me + step, n_dp)} for step in range(1, n_dp)]
    else:
        peers += [{"dp": lax.rem(me + 2 * step, n_dp)} for step in range(1, n_dp // 2)]
        peers += [{"dp": flip(me)}]
    for peer in peers:
        pl.semaphore_signal(barrier, inc=1, device_id=peer, device_id_type=MESH)
    pl.semaphore_wait(barrier, len(peers))


def send(src, dst, send_sem, recv_sem, device):
    copy = pltpu.make_async_remote_copy(
        src_ref=src,
        dst_ref=dst,
        send_sem=send_sem,
        recv_sem=recv_sem,
        device_id=device,
        device_id_type=MESH,
    )
    copy.start()
    return copy


class Gather:
    def __init__(self, axis, count, me, full, sems):
        self.axis, self.count, self.me, self.full, self.sems = axis, count, me, full, sems
        self.n_outer = count // 2
        self.first, self.second = {}, {}
        for step in range(1, self.n_outer):
            peer = {axis: lax.rem(me + 2 * step, count)}
            self.first[step] = send(
                full.at[me], full.at[me], sems.at[0, step], sems.at[1, step], peer
            )
        self.hand_on(0, me)

    def hand_on(self, step, block):
        self.second[step] = send(
            self.full.at[block],
            self.full.at[block],
            self.sems.at[2, step],
            self.sems.at[3, step],
            {self.axis: flip(self.me)},
        )

    def forward(self, step):
        self.first[step].wait_recv()
        self.hand_on(step, lax.rem(self.me + self.count - 2 * step, self.count))

    def arrive(self):
        for copy in self.second.values():
            copy.wait_recv()

    def leave(self):
        for copy in list(self.first.values()) + list(self.second.values()):
            copy.wait_send()

    def finish(self):
        self.arrive()
        self.leave()


class Reduce:
    def __init__(self, axis, count, me, parts, pair, sums, far, sems):
        self.axis, self.count, self.me, self.parts = axis, count, me, parts
        self.pair, self.sums, self.far, self.sems = pair, sums, far, sems
        self.n_outer = count // 2
        self.first, self.second = {}, {}
        for step in list(range(1, self.n_outer)) + [0]:
            block = lax.rem(flip(me) + 2 * step, count)
            self.first[step] = send(
                parts.at[block], pair.at[step], sems.at[0, step], sems.at[1, step],
                {axis: flip(me)},
            )

    def forward(self, step):
        self.first[step].wait_recv()
        peer = lax.rem(self.me + 2 * step, self.count)
        self.sums[step] = (
            self.parts[peer].astype(jnp.float32) + self.pair[step].astype(jnp.float32)
        ).astype(jnp.bfloat16)
        self.second[step] = send(
            self.sums.at[step],
            self.far.at[step],
            self.sems.at[2, step],
            self.sems.at[3, step],
            {self.axis: peer},
        )

    def total(self):
        self.first[0].wait_recv()
        total = self.parts[self.me].astype(jnp.float32) + self.pair[0].astype(jnp.float32)
        for step in range(1, self.n_outer):
            self.second[step].wait_recv()
            total = total + self.far[step].astype(jnp.float32)
        return total

    def finish(self):
        for copy in list(self.first.values()) + list(self.second.values()):
            copy.wait_send()


def forward_all(stages, first=1):
    last = max(stage.n_outer for stage in stages)
    for step in range(first, last):
        for stage in stages:
            if step not in stage.second and step < stage.n_outer:
                stage.forward(step)


def gather_kernel(
    n_dp, n_t, lengths_ref, w_ref, x_ref, cot_ref,
    qkv_all, wo_all, attn_all, grad_all, gain_one, gain_two,
    w_all, x_all, cot_all, units, w_sems, x_sems, cot_sems,
):
    me, rank = lax.axis_index("dp"), lax.axis_index("tensor")
    w_all[me] = w_ref[...]
    x_all[rank] = x_ref[...]
    cot_all[rank] = cot_ref[...]
    greet(n_dp, n_t, me, rank)
    weights = Gather("dp", n_dp, me, w_all, w_sems)
    x_rows = Gather("tensor", n_t, rank, x_all, x_sems)
    cot_rows = Gather("tensor", n_t, rank, cot_all, cot_sems)
    weights.forward(1)
    forward_all([x_rows, cot_rows])
    forward_all([weights])
    x_rows.arrive()
    cot_rows.arrive()
    row_count, width = x_ref.shape
    for block in range(n_t):
        unit, unused_inverse = unit_rows(x_all[block].astype(jnp.float32))
        units[block] = unit
        valid = valid_mask(lengths_ref, block * row_count, row_count)
        grad_all[block] = (valid * cot_all[block].astype(jnp.float32)).astype(jnp.bfloat16)
    weights.arrive()
    gains = jnp.sum(w_all[:, :GAIN_ROWS, :width].astype(jnp.float32), axis=0)
    gain_one[...] = gains[0:1]
    gain_two[...] = gains[1:2]
    for block in range(n_t):
        attn_all[block] = (units[block] * gains[0:1]).astype(jnp.bfloat16)
    split = qkv_all.shape[2]
    qkv_all[...] = w_all[:, GAIN_ROWS:, :split]
    wo_all[...] = w_all[:, GAIN_ROWS:, split:]
    x_rows.leave()
    cot_rows.leave()
    weights.leave()


def middle_kernel(
    n_dp, n_t, w_ref, part_ref, x_ref, gain_ref, w_all, residual_ref, mlp_all,
    pair, sums, far, w_sems, part_sems, row_sems,
):
    me, rank = lax.axis_index("dp"), lax.axis_index("tensor")
    w_all[me] = w_ref[...]
    greet(n_dp, n_t, me, rank)
    parts = Reduce("tensor", n_t, rank, part_ref, pair, sums, far, part_sems)
    weights = Gather("dp", n_dp, me, w_all, w_sems)
    forward_all([parts])
    weights.forward(1)
    residual = x_ref[...].astype(jnp.float32) + parts.total()
    residual_ref[...] = residual
    unit, unused_inverse = unit_rows(residual)
    mlp_all[rank] = (unit * gain_ref[...]).astype(jnp.bfloat16)
    rows = Gather("tensor", n_t, rank, mlp_all, row_sems)
    weights.forward(2)
    forward_all([rows])
    forward_all([weights])
    rows.finish()
    parts.finish()
    weights.finish()


def turn_kernel(
    n_dp, n_t, lengths_ref, grads, back_ref, out_part_ref, residual_ref, gain_ref,
    cot_ref,
    w_sum, output_ref, grad_residual_ref, grad_all, gain_part,
    back_pair, back_sums, back_far, out_pair, out_sums, out_far, pair, sums, far,
    back_sems, out_sems, w_sems, row_sems,
):
    me, rank = lax.axis_index("dp"), lax.axis_index("tensor")
    greet(n_dp, n_t, me, rank)
    back = Reduce("tensor", n_t, rank, back_ref, back_pair, back_sums, back_far, back_sems)
    weights = Reduce("dp", n_dp, me, grads, pair, sums, far, w_sems)
    forward_all([back])
    mlp_out = Reduce("tensor", n_t, rank, out_part_ref, out_pair, out_sums, out_far, out_sems)
    weights.forward(1)
    grad = back.total()
    residual = residual_ref[...]
    row_count = residual.shape[0]
    valid = valid_mask(lengths_ref, rank * row_count, row_count)
    unit, inverse = unit_rows(residual)
    gain_part[...] = jnp.sum(grad * unit, axis=0, keepdims=True)
    grad_residual = valid * cot_ref[...].astype(jnp.float32) + norm_back(
        unit, inverse, gain_ref[...], grad
    )
    grad_residual_ref[...] = grad_residual
    grad_all[rank] = grad_residual.astype(jnp.bfloat16)
    rows = Gather("tensor", n_t, rank, grad_all, row_sems)
    weights.forward(2)
    forward_all([mlp_out])
    forward_all([rows])
    forward_all([weights])
    output_ref[...] = (valid * (residual + mlp_out.total())).astype(jnp.bfloat16)
    rows.finish()
    back.finish()
    mlp_out.finish()
    w_sum[...] = weights.total()
    weights.finish()


def last_kernel(
    n_dp, n_t, grads, back_ref, x_ref, gain_ref, grad_residual_ref, gain_part_ref,
    w_sum, input_grad_ref, gain_sum_ref,
    back_pair, back_sums, back_far, pair, sums, far, own_gain, near_gain, group_gain, far_gain,
    back_sems, w_sems, near_sems, far_sems,
):
    me, rank = lax.axis_index("dp"), lax.axis_index("tensor")
    greet(n_dp, n_t, me, rank, all_dp=True)
    back = Reduce("tensor", n_t, rank, back_ref, back_pair, back_sums, back_far, back_sems)
    weights = Reduce("dp", n_dp, me, grads, pair, sums, far, w_sems)
    forward_all([back])
    weights.forward(1)
    grad = back.total()
    unit, inverse = unit_rows(x_ref[...].astype(jnp.float32))
    width = unit.shape[1]
    own_gain[0:1, :] = jnp.sum(grad * unit, axis=0, keepdims=True)
    own_gain[1:2, :] = gain_part_ref[...]
    own_gain[2:8, :] = jnp.zeros((6, width), jnp.float32)
    near = [
        send(own_gain, near_gain.at[step - 1], near_sems.at[0, step], near_sems.at[1, step],
             {"tensor": lax.rem(rank + step, n_t)})
        for step in range(1, n_t)
    ]
    weights.forward(2)
    input_grad_ref[...] = (
        grad_residual_ref[...] + norm_back(unit, inverse, gain_ref[...], grad)
    ).astype(jnp.bfloat16)
    total = own_gain[...]
    for step in range(1, n_t):
        near[step - 1].wait_recv()
        total = total + near_gain[step - 1]
    group_gain[...] = total
    far_copies = [
        send(group_gain, far_gain.at[step - 1], far_sems.at[0, step], far_sems.at[1, step],
             {"dp": lax.rem(me + step, n_dp)})
        for step in range(1, n_dp)
    ]
    forward_all([weights])
    for step in range(1, n_dp):
        far_copies[step - 1].wait_recv()
        total = total + far_gain[step - 1]
    gain_sum_ref[...] = total
    for copy in near + far_copies:
        copy.wait_send()
    back.finish()
    w_sum[...] = weights.total()
    weights.finish()


def call(kernel, n_dp, n_t, number, outs, scratch, operands):
    in_vmem = pl.BlockSpec(memory_space=pltpu.VMEM)
    moved = sum(op.size * op.dtype.itemsize for op in operands)
    return pl.pallas_call(
        functools.partial(kernel, n_dp, n_t),
        out_shape=[jax.ShapeDtypeStruct(shape, kind) for shape, kind in outs],
        in_specs=[
            pl.BlockSpec(memory_space=pltpu.SMEM) if op.dtype == jnp.int32 else in_vmem
            for op in operands
        ],
        out_specs=[in_vmem] * len(outs),
        scratch_shapes=scratch,
        compiler_params=pltpu.CompilerParams(
            collective_id=number, has_side_effects=True, vmem_limit_bytes=40 * 2**20
        ),
        cost_estimate=pl.CostEstimate(flops=0, bytes_accessed=2 * moved, transcendentals=0),
    )(*operands)


def dot(first, second, dims):
    return lax.dot_general(first, second, (dims, ((), ())), preferred_element_type=jnp.float32)


def shards(inputs, seq_lengths, attn_gain, wqkv, wo, mlp_gain, wi, wo2, cotangent):
    low = jnp.bfloat16
    n_dp, n_t = lax.axis_size("dp"), lax.axis_size("tensor")
    me, rank = lax.axis_index("dp"), lax.axis_index("tensor")
    local_rows, width = inputs.shape
    group_rows = local_rows * n_t
    depth = wqkv.shape[0]
    head_cols = wqkv.shape[2]
    heads_here = head_cols // HEAD_DIM
    hidden_cols = wi.shape[2]
    first_cols = 3 * head_cols + wo.shape[0]
    second_cols = 2 * hidden_cols + wo2.shape[0]
    n_outer = n_dp // 2

    def dma(count):
        return pltpu.SemaphoreType.DMA(count)

    def row_sems():
        return dma((4, n_t // 2))

    segment, position = layout(seq_lengths[0], group_rows)
    cosine, sine_table = rotation(position)

    gain_block = lax.dynamic_update_slice(
        jnp.zeros((GAIN_ROWS, first_cols), low), jnp.stack([attn_gain, mlp_gain]), (0, me * depth)
    )
    first_block = jnp.concatenate(
        [gain_block, jnp.concatenate([wqkv.reshape(depth, 3 * head_cols), wo.T], axis=1)], axis=0
    )
    second_block = jnp.concatenate([wi.reshape(depth, 2 * hidden_cols), wo2.T], axis=1)

    row_block = (n_t, local_rows, width)
    full_qkv, full_wo, attn_all, grad_mlp_all, gain_one, gain_two = call(
        gather_kernel, n_dp, n_t, 1,
        [
            ((n_dp, depth, 3 * head_cols), low),
            ((n_dp, depth, wo.shape[0]), low),
            (row_block, low),
            (row_block, low),
            ((1, width), jnp.float32),
            ((1, width), jnp.float32),
        ],
        [
            pltpu.VMEM((n_dp,) + first_block.shape, low),
            pltpu.VMEM(row_block, low),
            pltpu.VMEM(row_block, low),
            pltpu.VMEM(row_block, jnp.float32),
            dma((4, n_outer)), row_sems(), row_sems(),
        ],
        (seq_lengths, first_block, inputs, cotangent),
    )
    full_qkv = full_qkv.reshape(width, 3 * head_cols)
    full_wo = full_wo.reshape(width, wo.shape[0])
    attn_all = attn_all.reshape(group_rows, width)
    grad_mlp_all = grad_mlp_all.reshape(group_rows, width)
    qkv = dot(attn_all, full_qkv, ((1,), (0,))).reshape(group_rows, 3, heads_here, HEAD_DIM)
    query_low = rotate(qkv[:, 0], cosine, sine_table).astype(low)
    key_low = rotate(qkv[:, 1], cosine, sine_table).astype(low)
    value_low = qkv[:, 2].astype(low)
    scores = (
        jnp.einsum("qhd,khd->hqk", query_low, key_low, preferred_element_type=jnp.float32)
        * SCORE_SCALE
    )
    scores = jnp.where((segment[:, None] == segment[None, :])[None], scores, -1e30)
    exponent = jnp.exp(scores - jnp.max(scores, axis=-1, keepdims=True))
    probs = exponent / jnp.sum(exponent, axis=-1, keepdims=True)
    prob_low = probs.astype(low)
    context = (
        jnp.einsum("hqk,khd->qhd", prob_low, value_low, preferred_element_type=jnp.float32)
        .astype(low)
        .reshape(group_rows, head_cols)
    )
    attn_part = dot(context, full_wo, ((1,), (1,))).astype(low)

    slots = [pltpu.VMEM((n_t // 2, local_rows, width), low)] * 3
    second_all, residual, mlp_all = call(
        middle_kernel, n_dp, n_t, 2,
        [
            ((n_dp,) + second_block.shape, low),
            ((local_rows, width), jnp.float32),
            (row_block, low),
        ],
        slots + [dma((4, n_outer)), row_sems(), row_sems()],
        (second_block, attn_part.reshape(row_block), inputs, gain_two),
    )
    full_wi = second_all[:, :, : 2 * hidden_cols].reshape(width, 2 * hidden_cols)
    full_wo2 = second_all[:, :, 2 * hidden_cols :].reshape(width, wo2.shape[0])
    mlp_all = mlp_all.reshape(group_rows, width)
    projected = dot(mlp_all, full_wi, ((1,), (0,)))
    gate, other = projected[:, :hidden_cols], projected[:, hidden_cols:]
    bell = 0.5 * (1.0 + lax.erf(gate * 0.7071067811865476))
    gelu = gate * bell
    slope = bell + gate * jnp.exp(-0.5 * gate * gate) * 0.3989422804014327
    hidden = (gelu * other).astype(low)
    out_part = dot(hidden, full_wo2, ((1,), (1,))).astype(low)
    grad_hidden = dot(grad_mlp_all, full_wo2, ((1,), (0,)))
    grad_proj = jnp.concatenate(
        [grad_hidden * other * slope, grad_hidden * gelu], axis=1
    ).astype(low)
    back_part = dot(grad_proj, full_wi, ((1,), (1,))).astype(low)
    wi_grad = dot(mlp_all, grad_proj, ((0,), (0,))).astype(low)
    wo2_grad = dot(grad_mlp_all, hidden, ((0,), (0,))).astype(low)

    def reduce_scratch(cols):
        return [pltpu.VMEM((n_outer, depth, cols), low)] * 3

    second_sum, output, grad_residual, grad_all, gain_part = call(
        turn_kernel, n_dp, n_t, 3,
        [
            ((depth, second_cols), jnp.float32),
            ((local_rows, width), low),
            ((local_rows, width), jnp.float32),
            (row_block, low),
            ((1, width), jnp.float32),
        ],
        slots + slots + reduce_scratch(second_cols)
        + [row_sems(), row_sems(), dma((4, n_outer)), row_sems()],
        (
            seq_lengths,
            jnp.concatenate([wi_grad, wo2_grad], axis=1).reshape(n_dp, depth, second_cols),
            back_part.reshape(row_block), out_part.reshape(row_block),
            residual, gain_two, cotangent,
        ),
    )
    grad_all = grad_all.reshape(group_rows, width)
    grad_context = dot(grad_all, full_wo, ((1,), (0,))).astype(low)
    grad_context = grad_context.reshape(group_rows, heads_here, HEAD_DIM)
    grad_value = jnp.einsum(
        "hqk,qhd->khd", prob_low, grad_context, preferred_element_type=jnp.float32
    )
    grad_probs = jnp.einsum(
        "qhd,khd->hqk", grad_context, value_low, preferred_element_type=jnp.float32
    )
    row_inner = jnp.sum(probs * grad_probs, axis=-1, keepdims=True)
    grad_scores = (probs * (grad_probs - row_inner)).astype(low)
    grad_query = (
        jnp.einsum("hqk,khd->qhd", grad_scores, key_low, preferred_element_type=jnp.float32)
        * SCORE_SCALE
    )
    grad_key = (
        jnp.einsum("hqk,qhd->khd", grad_scores, query_low, preferred_element_type=jnp.float32)
        * SCORE_SCALE
    )
    grad_qkv = jnp.stack(
        [
            rotate(grad_query, cosine, -sine_table),
            rotate(grad_key, cosine, -sine_table),
            grad_value,
        ],
        axis=1,
    )
    grad_qkv = grad_qkv.astype(low).reshape(group_rows, 3 * head_cols)
    wqkv_grad = dot(attn_all, grad_qkv, ((0,), (0,))).astype(low)
    wo_grad = dot(grad_all, context, ((0,), (0,))).astype(low)
    attn_back = dot(grad_qkv, full_qkv, ((1,), (1,))).astype(low)

    gain_block_f32 = pltpu.VMEM((8, width), jnp.float32)
    first_sum, input_grad, gain_sum = call(
        last_kernel, n_dp, n_t, 4,
        [
            ((depth, first_cols), jnp.float32),
            ((local_rows, width), low),
            ((8, width), jnp.float32),
        ],
        slots + reduce_scratch(first_cols)
        + [
            gain_block_f32,
            pltpu.VMEM((n_t - 1, 8, width), jnp.float32),
            gain_block_f32,
            pltpu.VMEM((n_dp - 1, 8, width), jnp.float32),
            row_sems(), dma((4, n_outer)), dma((2, n_t)), dma((2, n_dp)),
        ],
        (
            jnp.concatenate([wqkv_grad, wo_grad], axis=1).reshape(n_dp, depth, first_cols),
            attn_back.reshape(row_block), inputs, gain_one, grad_residual, gain_part,
        ),
    )
    gains_here = lax.dynamic_slice_in_dim(gain_sum[:2], me * depth, depth, axis=1)
    return (
        output,
        input_grad,
        gains_here[0],
        first_sum[:, : 3 * head_cols].reshape(depth, 3, head_cols),
        first_sum[:, 3 * head_cols :].T,
        gains_here[1],
        second_sum[:, : 2 * hidden_cols].reshape(depth, 2, hidden_cols),
        second_sum[:, 2 * hidden_cols :].T,
    )


def solution(mesh):
    in_specs = (
        P(("dp", "tensor"), None),
        P("dp", None),
        P("dp"),
        P("dp", None, "tensor"),
        P("tensor", "dp"),
        P("dp"),
        P("dp", None, "tensor"),
        P("tensor", "dp"),
        P(("dp", "tensor"), None),
    )
    out_specs = (
        P(("dp", "tensor"), None),
        P(("dp", "tensor"), None),
        P("dp"),
        P("dp", None, "tensor"),
        P("tensor", "dp"),
        P("dp"),
        P("dp", None, "tensor"),
        P("tensor", "dp"),
    )
    return jax.shard_map(shards, mesh=mesh, in_specs=in_specs, out_specs=out_specs, check_vma=False)
```
